256 devices in a mesh: context: 64 (over z, y, core), dp: 4 (over x).
Axes of the slice: x: 4, y: 4, z: 8, core: 2. Of those that a mesh axis runs over, the one named last changes fastest.
Arguments:
- tokens: bfloat16 [4, 16384, 8192], P('dp', 'context'), may hold values from -16 to 16
- projection: bfloat16 [8192, 1280], P(('context', 'dp')), may hold values from -0.09375 to 0.09375
- doc_lengths: int32 [4, 6], P('dp'), may hold values from 1 to 8192, 16384 in all within a row
Outputs:
- attended: bfloat16 [4, 16384, 1024], P('dp', 'context')
The draws below stay inside these ranges and needn't reach their ends.
Inputs may be any that keep to these rules, and one draw needn't show every extreme that they name: `doc_lengths`: each row's lengths sum to 16384, and some document has exactly 8192 tokens.
All inputs are finite; a program needn't handle non-finite values.
Results may differ from the reference program's by a relative error of at most 0.007.
The reference program's roundings to bfloat16 on the way count: a program that leaves them out, or rounds other values in their place, can miss the bound.
Values may be sent and summed in bfloat16 or wider, within the bound.
No kernel may reach another device: no remote copies, remote signals or barrier semaphores. Data moves between devices by JAX's collectives and lax.ppermute only.
A program may use at most 64 MiB of HBM per device.

```python
import math
import jax
import jax.numpy as jnp
import numpy as np
from jax import lax

D = 8192
HEADS = 8
HEAD = 128
TOK_DEV = 256
DOCS = 6
SEQ = 16384
DOC_MOST = 8192
REACH = 32
COLS = 1280
N_DP = 4


def draw_tokens(key, part):
    key = jax.random.fold_in(key, 11)
    first = jax.random.fold_in(key, 0)
    shape = (N_DP, SEQ, D)
    values = jax.random.normal(first, shape, jnp.float32)
    return jnp.clip(values, -4.0, 4.0).astype(jnp.bfloat16)


def shard_levels(rng, shape, shards, least, top_value):
    factor_of, own = 1.0, jax.random.fold_in(rng, 6)
    for position, blocks in shards:
        steps = jnp.exp(jax.random.uniform(jax.random.fold_in(own, position), (blocks,), jnp.float32, least / len(shards), top_value / len(shards)))
        factor_of = factor_of * jnp.repeat(steps, shape[position] // blocks).reshape([-1 if axis == position else 1 for axis in range(len(shape))])
    return factor_of


def split_up(number_of, total, bound, slope):
    weights = [(1 << 20) // math.isqrt(rank ** slope) + 1 for rank in range(2, number_of + 1)]
    rest, holding = total - bound - (number_of - 1), [1] * (number_of - 1)
    while rest > 0:
        candidates = [i for i in range(number_of - 1) if holding[i] < bound]
        whole, remaining = sum([weights[i] for i in candidates]), rest
        for i in candidates:
            more = min(bound - holding[i], max(1, remaining * weights[i] // whole), rest)
            holding[i] = holding[i] + more
            rest = rest - more
    return np.array([bound] + holding)


def uneven(stream_key, count, total, bound, slope):
    if count == 2:
        one = jax.random.randint(stream_key, (), max(1, total - bound), min(bound, total - 1) + 1)
        return jnp.stack([one, total - one])
    tallies = jnp.asarray(split_up(count, total, bound, slope), jnp.int32)
    twos = (count - 1) // 2
    source_of, taker = tallies[1:1 + 2 * twos:2], tallies[2:2 + 2 * twos:2]
    room = jnp.minimum(source_of - 1, bound - taker)
    moved = jax.random.randint(jax.random.fold_in(stream_key, 1), (twos,), 0, 1 << 20) % (room + 1)
    tallies = tallies.at[1:1 + 2 * twos:2].set(source_of - moved).at[2:2 + 2 * twos:2].set(taker + moved)
    return tallies[jax.random.permutation(jax.random.fold_in(stream_key, 2), count)]


def scatter_about(stream_key, shape, width, reach, pieces=(), held_as=jnp.bfloat16):
    result = width * jax.random.normal(stream_key, shape, jnp.float32)
    if pieces:
        result = result * shard_levels(stream_key, shape, pieces, -0.22, 0.18)
    return jnp.clip(result, -reach, reach).astype(held_as)


def setup_inputs(seed: int = 0) -> dict:
    arg_keys = jax.random.split(jax.random.key(seed), 4)
    tokens = draw_tokens(jax.random.fold_in(arg_keys[3], 71), 0)
    projection = scatter_about(arg_keys[1], (D, COLS), (D // 2) ** -0.5, 0.09375, ((0, 256),))
    doc_lengths = jax.vmap(lambda own: uneven(own, DOCS, SEQ, DOC_MOST, 2))(jax.random.split(arg_keys[2], N_DP)).reshape((N_DP, DOCS)).astype(jnp.int32)
    return dict(tokens=tokens, projection=projection, doc_lengths=doc_lengths)


def doc_tables(lengths, tpos):
    ends = jnp.cumsum(lengths).astype(jnp.int32)
    after = tpos[:, None] >= ends[None, :]
    docid = jnp.sum(after.astype(jnp.int32), axis=1).astype(jnp.int32)
    begin = jnp.sum(jnp.where(after, lengths[None, :], 0), axis=1).astype(jnp.int32)
    return docid, begin


def rotate(vecs, pos):
    half = vecs.shape[-1] // 2
    expo = jnp.arange(half).astype(jnp.float32) * (2.0 / vecs.shape[-1])
    inv = jnp.power(jnp.float32(500000.0), -expo)
    angle = pos[:, None] * inv[None, :]
    cosine = jnp.cos(angle)[:, None, :]
    sine = jnp.sin(angle)[:, None, :]
    first = vecs[..., :half]
    second = vecs[..., half:]
    return jnp.concatenate([first * cosine - second * sine, second * cosine + first * sine], axis=-1)


def one_sequence(rows, projection, lengths):
    span = HEADS * HEAD
    proj = jnp.dot(rows, projection, preferred_element_type=jnp.float32)
    tpos = jnp.arange(SEQ, dtype=jnp.int32)
    docid, begin = doc_tables(lengths, tpos)
    pos = (tpos - begin).astype(jnp.float32)
    queries = rotate(proj[:, :span].reshape(SEQ, HEADS, HEAD), pos).astype(jnp.bfloat16)
    keys = rotate(proj[:, span:span + HEAD].reshape(SEQ, 1, HEAD), pos).reshape(SEQ, HEAD).astype(jnp.bfloat16)
    values = proj[:, span + HEAD:].astype(jnp.bfloat16)
    window = (REACH + 1) * TOK_DEV
    scale = HEAD ** -0.5

    def block(index):
        qstart = (index * TOK_DEV).astype(jnp.int32)
        kstart = jnp.maximum(qstart - REACH * TOK_DEV, 0).astype(jnp.int32)
        qblock = lax.dynamic_slice_in_dim(queries, qstart, TOK_DEV, 0).astype(jnp.float32)
        kblock = lax.dynamic_slice_in_dim(keys, kstart, window, 0).astype(jnp.float32)
        vblock = lax.dynamic_slice_in_dim(values, kstart, window, 0).astype(jnp.float32)
        qtok = qstart + jnp.arange(TOK_DEV, dtype=jnp.int32)
        ktok = kstart + jnp.arange(window, dtype=jnp.int32)
        visible = (docid[ktok][None, :] == docid[qtok][:, None]) & (ktok[None, :] <= qtok[:, None])
        scores = jnp.einsum("qhd,kd->hqk", qblock, kblock) * scale
        scores = jnp.where(visible[None], scores, -1e30)
        top = jnp.max(scores, axis=-1, keepdims=True)
        weights = jnp.exp(scores - top) * visible[None].astype(jnp.float32)
        total = jnp.sum(weights, axis=-1)
        mixed = jnp.einsum("hqk,kd->hqd", weights, vblock) / total[..., None]
        return jnp.transpose(mixed, (1, 0, 2)).reshape(TOK_DEV, span).astype(jnp.bfloat16)

    blocks = lax.map(block, jnp.arange(SEQ // TOK_DEV, dtype=jnp.int32))
    return blocks.reshape(SEQ, span)


def reference(tokens, projection, doc_lengths):
    outputs = []
    for index in range(N_DP):
        outputs.append(one_sequence(tokens[index], projection, doc_lengths[index]))
    return jnp.stack(outputs, axis=0)
```

```python
import functools

import jax
import jax.numpy as jnp
import numpy as np
from jax import lax
from jax.experimental import pallas as pl
from jax.experimental.pallas import tpu as pltpu
from jax.sharding import PartitionSpec as P

HEADS = 8
HEAD = 128
REACH = 8192
KB = 1024
LOG2E = 1.4426950408889634


def doc_tables(lengths, tpos):
    ends = jnp.cumsum(lengths)
    after = tpos[:, None] >= ends[None, :]
    return jnp.sum(jnp.where(after, lengths[None, :], 0), axis=1).astype(jnp.int32)


def rotate(vecs, pos):
    half = vecs.shape[-1] // 2
    expo = jnp.arange(half).astype(jnp.float32) * (2.0 / vecs.shape[-1])
    inv = jnp.power(jnp.float32(500000.0), -expo)
    angle = pos[:, None] * inv[None, :]
    cosine = jnp.cos(angle)[:, None, :]
    sine = jnp.sin(angle)[:, None, :]
    first = vecs[..., :half]
    second = vecs[..., half:]
    return jnp.concatenate(
        [first * cosine - second * sine, second * cosine + first * sine], axis=-1
    )


def attend_kernel(heads, span_ref, begin_ref, q_ref, kv_hbm, out_ref, kvbuf, top, total, accum, sem):
    start, low, high, full_low, full_high = [span_ref[i] for i in range(5)]
    tok = q_ref.shape[0]
    factor = np.float32(HEAD**-0.5 * LOG2E)

    def fetch(i):
        return pltpu.make_async_copy(
            kv_hbm.at[pl.ds(pl.multiple_of(i * KB, KB), KB)], kvbuf.at[i - low], sem.at[i - low]
        )

    @pl.loop(low, high)
    def _(i):
        fetch(i).start()

    top[...] = jnp.full(top.shape, -1e30, jnp.float32)
    total[...] = jnp.zeros(total.shape, jnp.float32)
    accum[...] = jnp.zeros(accum.shape, jnp.float32)

    def block(i, masked):
        kv = kvbuf[i - low]
        keys = kv[:, :HEAD]
        values = kv[:, HEAD:]
        if masked:
            ktok = lax.broadcasted_iota(jnp.int32, (tok, KB), 1) + i * KB
            qtok = lax.broadcasted_iota(jnp.int32, (tok, KB), 0) + start
            visible = (ktok >= begin_ref[:, 0:1]) & (ktok <= qtok)
        for h in range(heads):
            scores = lax.dot_general(
                q_ref[:, h * HEAD : (h + 1) * HEAD],
                keys,
                (((1,), (1,)), ((), ())),
                preferred_element_type=jnp.float32,
            )
            if masked:
                scores = jnp.where(visible, scores, -1e30)
            old = top[h]
            new = jnp.maximum(old, jnp.max(scores, axis=1, keepdims=True))
            shrink = jnp.exp2((old - new) * factor)
            weights = jnp.exp2((scores - jnp.tile(new, (1, KB // HEAD))) * factor)
            top[h] = new
            total[h] = total[h] * shrink + jnp.sum(weights, axis=1, keepdims=True)
            accum[h] = accum[h] * shrink + jnp.dot(
                weights.astype(jnp.bfloat16), values, preferred_element_type=jnp.float32
            )

    @pl.loop(low, high)
    def _(i):
        fetch(i).wait()
        full = (i >= full_low) & (i < full_high)

        @pl.when(full)
        def _():
            block(i, False)

        @pl.when(jnp.logical_not(full))
        def _():
            block(i, True)

    for h in range(heads):
        out_ref[:, h * HEAD : (h + 1) * HEAD] = (accum[h] / total[h]).astype(jnp.bfloat16)


def attend(queries, keyval, begins, start):
    tok = queries.shape[0]
    heads = queries.shape[1] // HEAD
    slots = REACH // KB + 2
    spans = jnp.stack(
        [
            start,
            begins[0] // KB,
            (start + tok + KB - 1) // KB,
            (begins[-1] + KB - 1) // KB,
            (start + 1) // KB,
        ]
    ).astype(jnp.int32)
    vmem = pl.BlockSpec(memory_space=pltpu.VMEM)
    state = pltpu.VMEM((heads, tok, HEAD), jnp.float32)
    return pl.pallas_call(
        functools.partial(attend_kernel, heads),
        out_shape=jax.ShapeDtypeStruct((tok, heads * HEAD), jnp.bfloat16),
        in_specs=[
            pl.BlockSpec(memory_space=pltpu.SMEM),
            vmem,
            vmem,
            pl.BlockSpec(memory_space=pl.ANY),
        ],
        out_specs=vmem,
        scratch_shapes=[
            pltpu.VMEM((slots, KB, 2 * HEAD), jnp.bfloat16),
            state,
            state,
            state,
            pltpu.SemaphoreType.DMA((slots,)),
        ],
        compiler_params=pltpu.CompilerParams(vmem_limit_bytes=48 * 2**20),
        name="attend",
    )(spans, jnp.broadcast_to(begins[:, None], (tok, HEAD)), queries, keyval)


def per_device(tokens, projection, doc_lengths):
    tok = tokens.shape[1]
    rows = tokens[0]
    lengths = doc_lengths[0]
    span = HEADS * HEAD
    here = lax.axis_index("context")
    proj = jnp.dot(
        rows,
        lax.all_gather(projection, ("context", "dp"), axis=0, tiled=True),
        preferred_element_type=jnp.float32,
    )
    start = (here * tok).astype(jnp.int32)
    qtok = start + jnp.arange(tok, dtype=jnp.int32)
    begins = doc_tables(lengths, qtok)
    pos = (qtok - begins).astype(jnp.float32)
    rotated = rotate(proj[:, : span + HEAD].reshape(tok, HEADS + 1, HEAD), pos)
    rotated = rotated.reshape(tok, span + HEAD).astype(jnp.bfloat16)
    values = proj[:, span + HEAD :].astype(jnp.bfloat16)
    keyval = jnp.concatenate([rotated[:, span:], values], axis=1)
    everyone = lax.all_gather(keyval, "context", axis=0, tiled=True)
    return attend(rotated[:, :span], everyone, begins, start)[None]


def solution(mesh):
    in_specs = (P("dp", "context", None), P(("context", "dp"), None), P("dp", None))
    out_specs = P("dp", "context", None)
    return jax.shard_map(
        per_device, mesh=mesh, in_specs=in_specs, out_specs=out_specs, check_vma=False
    )
```

```python
import functools

import jax
import jax.numpy as jnp
import numpy as np
from jax import lax
from jax.experimental import pallas as pl
from jax.experimental.pallas import tpu as pltpu
from jax.sharding import Mesh
from jax.sharding import PartitionSpec as P

HEADS = 8
HEAD = 128
KB = 1024
LOG2E = 1.4426950408889634
NZ, NY, NX = 8, 4, 4
SIZE = {"z": NZ, "y": NY, "x": NX}
PLANES = 5
STEPS = (0, 1, -1, 2)


def doc_begins(lengths, tpos):
    ends = jnp.cumsum(lengths)
    after = tpos[:, None] >= ends[None, :]
    return jnp.sum(jnp.where(after, lengths[None, :], 0), axis=1).astype(jnp.int32)


def turn_tables(pos):
    expo = jnp.arange(HEAD // 2).astype(jnp.float32) * (2.0 / HEAD)
    inv = jnp.power(jnp.float32(500000.0), -expo)
    angle = pos[:, None] * inv[None, :]
    cosine, sine = jnp.cos(angle), jnp.sin(angle)
    return (
        jnp.concatenate([cosine, cosine], axis=1),
        jnp.concatenate([-sine, sine], axis=1),
    )


def shift(x, axis, by):
    size = SIZE[axis]
    return lax.ppermute(x, axis, [(i, (i + by) % size) for i in range(size)])


def swap(x):
    return lax.ppermute(x, "core", [(0, 1), (1, 0)])


def along_chips(x):
    wide = jnp.broadcast_to(x[None], (NZ,) + x.shape).reshape((2 * NZ,) + x.shape[1:])
    return lax.all_to_all(wide, ("z", "core"), 0, 0, tiled=True).reshape((NZ,) + x.shape)


def around(x, axis):
    return jnp.stack([x] + [shift(x, axis, by) for by in STEPS[1:]])


def around_last(x, axis):
    left, right = shift(x, axis, 1), shift(x, axis, -1)
    half = x.shape[0] // 2
    return [x, left, right, shift(left[:half], axis, 1), shift(right[half:], axis, -1)]


def project_kernel(orders, place_ref, cos_ref, sin_ref, own_hbm, other_hbm, *refs):
    jobs = len(orders)
    pieces = refs[: 5 * jobs]
    out_ref = refs[5 * jobs]
    rows, accum, rows_sem, sems = refs[5 * jobs + 1 : 5 * jobs + 5]
    weights = refs[5 * jobs + 5 :]
    mine, at_x, at_y = place_ref[0], place_ref[1], place_ref[2]
    tok = own_hbm.shape[0]
    copies = []
    for k, (src, core) in enumerate(((own_hbm, mine), (other_hbm, 1 - mine))):
        copies.append(
            pltpu.make_async_copy(src, rows.at[pl.ds(core * tok, tok)], rows_sem.at[k])
        )
    for job, order in enumerate(orders):
        for r in range(4):
            for j in range(4):
                if r < 3:
                    src = pieces[5 * job + r].at[j]
                else:
                    src = pieces[5 * job + 3 + j // 2].at[j % 2]
                if order == "yx":
                    y, x = at_y + (8 - STEPS[j]), at_x + (8 - STEPS[r])
                else:
                    y, x = at_y + (8 - STEPS[r]), at_x + (8 - STEPS[j])
                dst = weights[job].at[:, lax.rem(y, 4), :, lax.rem(x, 4)]
                copies.append(pltpu.make_async_copy(src, dst, sems.at[job, 4 * r + j]))
    for copy in copies:
        copy.start()
    for copy in copies:
        copy.wait()

    column = 0
    for job in range(jobs):
        wide = weights[job].shape[-1]
        accum[:, column : column + wide] = jnp.zeros((2 * tok, wide), jnp.float32)
        column += wide
    depth = 256 * NY

    @pl.loop(0, NZ)
    def _(z):
        left = rows[:, pl.ds(pl.multiple_of(z * depth, depth), depth)]
        column = 0
        for job in range(jobs):
            wide = weights[job].shape[-1]
            right = weights[job][z].reshape(depth, wide)
            accum[:, column : column + wide] += jnp.dot(
                left, right, preferred_element_type=jnp.float32
            )
            column += wide

    half = HEAD // 2
    for h in range(accum.shape[1] // HEAD):
        vecs = accum[:, h * HEAD : (h + 1) * HEAD]
        turned = jnp.concatenate([vecs[:, half:], vecs[:, :half]], axis=1)
        out_ref[:, h * HEAD : (h + 1) * HEAD] = (
            vecs * cos_ref[...] + turned * sin_ref[...]
        ).astype(jnp.bfloat16)


def project(place, tables, own, other, jobs, name):
    tok, depth = own.shape
    wides = [pieces[0].shape[-1] for _, pieces in jobs]
    flat = [piece for _, pieces in jobs for piece in pieces]
    vmem = pl.BlockSpec(memory_space=pltpu.VMEM)
    anywhere = pl.BlockSpec(memory_space=pl.ANY)
    return pl.pallas_call(
        functools.partial(project_kernel, [order for order, _ in jobs]),
        out_shape=jax.ShapeDtypeStruct((2 * tok, sum(wides)), jnp.bfloat16),
        in_specs=[pl.BlockSpec(memory_space=pltpu.SMEM), vmem, vmem]
        + [anywhere] * (2 + len(flat)),
        out_specs=vmem,
        scratch_shapes=[
            pltpu.VMEM((2 * tok, depth), jnp.bfloat16),
            pltpu.VMEM((2 * tok, sum(wides)), jnp.float32),
            pltpu.SemaphoreType.DMA((2,)),
            pltpu.SemaphoreType.DMA((len(jobs), 16)),
        ]
        + [pltpu.VMEM((NZ, NY, 2, NX, 32, wide), jnp.bfloat16) for wide in wides],
        compiler_params=pltpu.CompilerParams(vmem_limit_bytes=32 * 2**20),
        cost_estimate=pl.CostEstimate(
            flops=4 * tok * depth * sum(wides), bytes_accessed=2 * depth * (2 * tok + sum(wides)), transcendentals=0
        ),
        name=name,
    )(place, *tables, own, other, *flat)


def attend_kernel(heads, span_ref, begin_ref, q_ref, *refs):
    groups = refs[:4]
    out_ref, kv, top, total, accum, sem = refs[4:]
    start, base, low, high, full_low, full_high, mine, at_y = [span_ref[i] for i in range(8)]
    tok = q_ref.shape[0]
    factor = np.float32(HEAD**-0.5 * LOG2E)
    copies = []
    for k, src in enumerate(groups):
        which = mine if k < 2 else 1 - mine
        first = 0 if k % 2 == 0 else PLANES - src.shape[1]
        for r in range(4):
            y = lax.rem(at_y + (8 - STEPS[r]), 4)
            dst = kv.at[which, pl.ds(first, src.shape[1]), y]
            copies.append(pltpu.make_async_copy(src.at[r], dst, sem.at[k, r]))
    for copy in copies:
        copy.start()

    top[...] = jnp.full(top.shape, -1e30, jnp.float32)
    total[...] = jnp.zeros(total.shape, jnp.float32)
    accum[...] = jnp.zeros(accum.shape, jnp.float32)
    for copy in copies:
        copy.wait()
    parts = KB // tok
    rows = NY // parts

    def block(i, masked):
        here = pl.ds(lax.rem(i, rows) * parts, parts)
        keys = kv[0, i // rows, here].reshape(KB, HEAD)
        values = kv[1, i // rows, here].reshape(KB, HEAD)
        if masked:
            ktok = lax.broadcasted_iota(jnp.int32, (tok, KB), 1) + (base + i * KB)
            qtok = lax.broadcasted_iota(jnp.int32, (tok, KB), 0) + start
            visible = (ktok >= begin_ref[:, 0:1]) & (ktok <= qtok)
        for h in range(heads):
            scores = lax.dot_general(
                q_ref[:, h * HEAD : (h + 1) * HEAD],
                keys,
                (((1,), (1,)), ((), ())),
                preferred_element_type=jnp.float32,
            )
            if masked:
                scores = jnp.where(visible, scores, -1e30)
            old = top[h]
            new = jnp.maximum(old, jnp.max(scores, axis=1, keepdims=True))
            shrink = jnp.exp2((old - new) * factor)
            weights = jnp.exp2((scores - jnp.tile(new, (1, KB // HEAD))) * factor)
            top[h] = new
            total[h] = total[h] * shrink + jnp.sum(weights, axis=1, keepdims=True)
            accum[h] = accum[h] * shrink + jnp.dot(
                weights.astype(jnp.bfloat16), values, preferred_element_type=jnp.float32
            )

    @pl.loop(low, high)
    def _(i):
        full = (i >= full_low) & (i < full_high)

        @pl.when(full)
        def _():
            block(i, False)

        @pl.when(jnp.logical_not(full))
        def _():
            block(i, True)

    for h in range(heads):
        out_ref[:, h * HEAD : (h + 1) * HEAD] = (accum[h] / total[h]).astype(jnp.bfloat16)


def attend(queries, groups, begins, start, base, mine, at_y):
    tok = queries.shape[0]
    heads = queries.shape[1] // HEAD
    spans = jnp.stack(
        [
            start,
            base,
            lax.div(begins[0] - base, KB),
            lax.div(start - base + (tok + KB - 1), KB),
            lax.div(begins[-1] - base + (KB - 1), KB),
            lax.div(start - base + 1, KB),
            mine,
            at_y,
        ]
    ).astype(jnp.int32)
    vmem = pl.BlockSpec(memory_space=pltpu.VMEM)
    state = pltpu.VMEM((heads, tok, HEAD), jnp.float32)
    return pl.pallas_call(
        functools.partial(attend_kernel, heads),
        out_shape=jax.ShapeDtypeStruct((tok, heads * HEAD), jnp.bfloat16),
        in_specs=[pl.BlockSpec(memory_space=pltpu.SMEM), vmem, vmem]
        + [pl.BlockSpec(memory_space=pl.ANY)] * 4,
        out_specs=vmem,
        scratch_shapes=[
            pltpu.VMEM((2, PLANES, NY, tok, HEAD), jnp.bfloat16),
            state,
            state,
            state,
            pltpu.SemaphoreType.DMA((4, 4)),
        ],
        compiler_params=pltpu.CompilerParams(vmem_limit_bytes=48 * 2**20),
        name="attend",
    )(spans, jnp.broadcast_to(begins[:, None], (tok, HEAD)), queries, *groups)


def per_device(tokens, projection, doc_lengths):
    half = tokens.shape[1]
    tok = 2 * half
    lengths = doc_lengths[0]
    span = HEADS // 2 * HEAD
    mine, plane = lax.axis_index("core"), lax.axis_index("z")
    at_x, at_y = lax.axis_index("x"), lax.axis_index("y")
    own = tokens[0]
    other = swap(own)

    small = jnp.stack([projection[:, 2 * span :][:, :HEAD], projection[:, 2 * span + HEAD :]])
    big = jnp.stack([projection[:, :span], projection[:, span : 2 * span]])
    small = along_chips(small)
    small = around_last(around(small, "y"), "x")
    big = along_chips(big)
    left = around_last(around(big[..., : span // 2], "y"), "x")
    right = around_last(around(big[..., span // 2 :], "x"), "y")

    start = ((plane * NY + at_y) * tok).astype(jnp.int32)
    qtok = start + jnp.arange(tok, dtype=jnp.int32)
    begins = doc_begins(lengths, qtok)
    cosine, sine = turn_tables((qtok - begins).astype(jnp.float32))
    place = jnp.stack([mine, at_x, at_y]).astype(jnp.int32)

    keyed = mine == 0
    tables = jnp.where(keyed, cosine, 1.0), jnp.where(keyed, sine, 0.0)
    keyval = project(place, tables, own, other, [("yx", small)], "project_keyval")
    planes = [shift(keyval, "z", PLANES - 1 - p) for p in range(PLANES - 1)] + [keyval]
    early = around(jnp.stack(planes[:2]), "y")
    late = around(jnp.stack(planes[2:]), "y")
    groups = [early, late, swap(early), swap(late)]

    queries = project(
        place, (cosine, sine), own, other, [("yx", left), ("xy", right)], "project_queries"
    )
    base = ((plane - (PLANES - 1)) * (NY * tok)).astype(jnp.int32)
    mixed = attend(queries, groups, begins, start, base, mine, at_y).reshape(2, half, span)
    kept = lax.dynamic_index_in_dim(mixed, mine, 0, keepdims=False)
    given = swap(lax.dynamic_index_in_dim(mixed, 1 - mine, 0, keepdims=False))
    return jnp.where(
        keyed, jnp.concatenate([kept, given], axis=1), jnp.concatenate([given, kept], axis=1)
    )[None]


def solution(mesh):
    mesh = Mesh(mesh.devices.reshape(NZ, NY, 2, NX), ("z", "y", "core", "x"))
    everyone = ("z", "y", "core")
    in_specs = (P("x", everyone, None), P(everyone + ("x",), None), P("x", None))
    out_specs = P("x", everyone, None)
    return jax.shard_map(
        per_device, mesh=mesh, in_specs=in_specs, out_specs=out_specs, check_vma=False
    )
```

```python
import functools

import jax
import jax.numpy as jnp
import numpy as np
from jax import lax
from jax.experimental import pallas as pl
from jax.experimental.pallas import tpu as pltpu
from jax.sharding import Mesh
from jax.sharding import PartitionSpec as P

HEADS = 8
HEAD = 128
KB = 1024
LOG2E = 1.4426950408889634
NZ, NY, NX = 8, 4, 4
SIZE = {"z": NZ, "y": NY, "x": NX}
PLANES = 5
STEPS = (0, 1, -1, 2)
CHUNKS = 2


def doc_begins(lengths, tpos):
    ends = jnp.cumsum(lengths)
    after = tpos[:, None] >= ends[None, :]
    return jnp.sum(jnp.where(after, lengths[None, :], 0), axis=1).astype(jnp.int32)


def turn_tables(pos):
    expo = jnp.arange(HEAD // 2).astype(jnp.float32) * (2.0 / HEAD)
    inv = jnp.power(jnp.float32(500000.0), -expo)
    angle = pos[:, None] * inv[None, :]
    cosine, sine = jnp.cos(angle), jnp.sin(angle)
    return (
        jnp.concatenate([cosine, cosine], axis=1),
        jnp.concatenate([-sine, sine], axis=1),
    )


def shift(x, axis, by):
    size = SIZE[axis]
    return lax.ppermute(x, axis, [(i, (i + by) % size) for i in range(size)])


def swap(x):
    return lax.ppermute(x, "core", [(0, 1), (1, 0)])


def along_chips(x):
    wide = jnp.broadcast_to(x[None], (NZ,) + x.shape).reshape((2 * NZ,) + x.shape[1:])
    return lax.all_to_all(wide, ("z", "core"), 0, 0, tiled=True).reshape((NZ,) + x.shape)


def spread(x, axis):
    wide = jnp.broadcast_to(x[None], (SIZE[axis],) + x.shape)
    return lax.all_to_all(wide, axis, 0, 0, tiled=True)


def around(x, axis):
    return jnp.stack([x] + [shift(x, axis, by) for by in STEPS[1:]])


def around_last(x, axis):
    left, right = shift(x, axis, 1), shift(x, axis, -1)
    half = x.shape[0] // 2
    return [x, left, right, shift(left[:half], axis, 1), shift(right[half:], axis, -1)]


def blocks_of(kind, pieces, at_y, at_x):
    if kind == "x, then y":
        return [
            (pieces[0].at[y, j], y, lax.rem(at_x + (8 - STEPS[j]), 4))
            for y in range(NY)
            for j in range(NX)
        ]
    found = []
    for r in range(4):
        for j in range(4):
            whole = r < 3 or len(pieces) == 4
            src = pieces[r].at[j] if whole else pieces[3 + j // 2].at[j % 2]
            y = j if kind == "ordered y, then x" else lax.rem(at_y + (8 - STEPS[j]), 4)
            found.append((src, y, lax.rem(at_x + (8 - STEPS[r]), 4)))
    return found


def project_kernel(kinds, counts, place_ref, cos_ref, sin_ref, own_hbm, other_hbm, *refs):
    jobs = len(kinds)
    pieces = [refs[sum(counts[:job]) : sum(counts[: job + 1])] for job in range(jobs)]
    out_ref, rows, accum, rows_sem, sems = refs[sum(counts) : sum(counts) + 5]
    weights = refs[sum(counts) + 5]
    wides = [piece[0].shape[-1] for piece in pieces]
    mine, at_x, at_y = place_ref[0], place_ref[1], place_ref[2]
    tok = own_hbm.shape[0]
    thick = NZ // CHUNKS
    wide_depth = 256 * NY * thick

    def fetch(chunk):
        planes = pl.ds(chunk * thick, thick)
        deep = pl.ds(chunk * wide_depth, wide_depth)
        copies = []
        for job, kind in enumerate(kinds):
            for n, (src, y, x) in enumerate(blocks_of(kind, pieces[job], at_y, at_x)):
                columns = pl.ds(sum(wides[:job]), wides[job])
                dst = weights.at[planes, y, :, x, :, columns]
                copies.append(pltpu.make_async_copy(src.at[planes], dst, sems.at[chunk, job, n]))
        for k, (src, core) in enumerate(((own_hbm, mine), (other_hbm, 1 - mine))):
            dst = rows.at[pl.ds(pl.multiple_of(core * tok, tok), tok), deep]
            copies.append(pltpu.make_async_copy(src.at[:, deep], dst, rows_sem.at[chunk, k]))
        return copies

    chunks = [fetch(chunk) for chunk in range(CHUNKS)]
    for copies in chunks:
        for copy in copies:
            copy.start()
    accum[...] = jnp.zeros(accum.shape, jnp.float32)
    depth = 256 * NY
    for chunk, copies in enumerate(chunks):
        for copy in copies:
            copy.wait()

        @pl.loop(chunk * thick, (chunk + 1) * thick)
        def _(z):
            left = rows[:, pl.ds(pl.multiple_of(z * depth, depth), depth)]
            right = weights[z].reshape(depth, sum(wides))
            accum[...] += jnp.dot(left, right, preferred_element_type=jnp.float32)

    half = HEAD // 2
    for h in range(accum.shape[1] // HEAD):
        vecs = accum[:, h * HEAD : (h + 1) * HEAD]
        turned = jnp.concatenate([vecs[:, half:], vecs[:, :half]], axis=1)
        out_ref[:, h * HEAD : (h + 1) * HEAD] = (
            vecs * cos_ref[...] + turned * sin_ref[...]
        ).astype(jnp.bfloat16)


def project(place, tables, own, other, jobs, name):
    tok, depth = own.shape
    wides = [pieces[0].shape[-1] for _, pieces in jobs]
    flat = [piece for _, pieces in jobs for piece in pieces]
    vmem = pl.BlockSpec(memory_space=pltpu.VMEM)
    anywhere = pl.BlockSpec(memory_space=pltpu.HBM)
    return pl.pallas_call(
        functools.partial(
            project_kernel, [kind for kind, _ in jobs], [len(pieces) for _, pieces in jobs]
        ),
        out_shape=jax.ShapeDtypeStruct((2 * tok, sum(wides)), jnp.bfloat16),
        in_specs=[pl.BlockSpec(memory_space=pltpu.SMEM), vmem, vmem]
        + [anywhere] * (2 + len(flat)),
        out_specs=vmem,
        scratch_shapes=[
            pltpu.VMEM((2 * tok, depth), jnp.bfloat16),
            pltpu.VMEM((2 * tok, sum(wides)), jnp.float32),
            pltpu.SemaphoreType.DMA((CHUNKS, 2)),
            pltpu.SemaphoreType.DMA((CHUNKS, len(jobs), 16)),
            pltpu.VMEM((NZ, NY, 2, NX, 32, sum(wides)), jnp.bfloat16),
        ],
        compiler_params=pltpu.CompilerParams(vmem_limit_bytes=58 * 2**20),
        cost_estimate=pl.CostEstimate(
            flops=4 * tok * depth * sum(wides),
            bytes_accessed=2 * depth * (2 * tok + sum(wides)),
            transcendentals=0,
        ),
        name=name,
    )(place, *tables, own, other, *flat)


def attend_kernel(heads, span_ref, begin_ref, q_ref, *refs):
    groups = refs[:4]
    out_ref, kv, top, total, accum, sem = refs[4:]
    start, base, low, high, full_low, full_high, mine = [span_ref[i] for i in range(7)]
    tok = q_ref.shape[0]
    factor = np.float32(HEAD**-0.5 * LOG2E)
    copies = []
    for k, src in enumerate(groups):
        which = mine if k < 2 else 1 - mine
        first = 0 if k % 2 == 0 else PLANES - src.shape[1]
        for r in range(4):
            dst = kv.at[which, pl.ds(first, src.shape[1]), r]
            copies.append(pltpu.make_async_copy(src.at[r], dst, sem.at[k, r]))
    for copy in copies[4:8] + copies[12:] + copies[:4] + copies[8:12]:
        copy.start()

    top[...] = jnp.full(top.shape, -1e30, jnp.float32)
    total[...] = jnp.zeros(total.shape, jnp.float32)
    accum[...] = jnp.zeros(accum.shape, jnp.float32)
    for copy in copies[4:8] + copies[12:]:
        copy.wait()
    parts = KB // tok
    rows = NY // parts
    early = rows * groups[0].shape[1]
    ones = jnp.ones((KB, HEAD), jnp.bfloat16)

    def block(i, masked):
        here = pl.ds(lax.rem(i, rows) * parts, parts)
        keys = kv[0, i // rows, here].reshape(KB, HEAD)
        values = jnp.concatenate([kv[1, i // rows, here].reshape(KB, HEAD), ones], axis=1)
        if masked:
            ktok = lax.broadcasted_iota(jnp.int32, (tok, KB), 1) + (base + i * KB)
            qtok = lax.broadcasted_iota(jnp.int32, (tok, KB), 0) + start
            visible = (ktok >= begin_ref[:, 0:1]) & (ktok <= qtok)

        def score(h):
            return lax.dot_general(
                q_ref[:, h * HEAD : (h + 1) * HEAD],
                keys,
                (((1,), (1,)), ((), ())),
                preferred_element_type=jnp.float32,
            )

        following = score(0)
        for h in range(heads):
            scores = following
            if h + 1 < heads:
                following = score(h + 1)
            if masked:
                scores = jnp.where(visible, scores, -1e30)
            old = top[h]
            new = jnp.maximum(old, jnp.max(scores, axis=1, keepdims=True))
            shrink = jnp.exp2((old - new) * factor)
            weights = jnp.exp2((scores - jnp.tile(new, (1, KB // HEAD))) * factor)
            top[h] = new
            sums = jnp.dot(weights.astype(jnp.bfloat16), values, preferred_element_type=jnp.float32)
            total[h] = total[h] * shrink + sums[:, HEAD:]
            accum[h] = accum[h] * shrink + sums[:, :HEAD]

    def wait_early():
        for copy in copies[:4] + copies[8:12]:
            copy.wait()

    @pl.loop(0, high - low)
    def _(n):
        i = high - 1 - n
        full = (i >= full_low) & (i < full_high)

        @pl.when(i == early - 1)
        def _():
            wait_early()

        @pl.when(full)
        def _():
            block(i, False)

        @pl.when(jnp.logical_not(full))
        def _():
            block(i, True)

    @pl.when(low >= early)
    def _():
        wait_early()

    for h in range(heads):
        out_ref[:, h * HEAD : (h + 1) * HEAD] = (accum[h] / total[h]).astype(jnp.bfloat16)


def attend(queries, groups, begins, start, base, mine):
    tok = queries.shape[0]
    heads = queries.shape[1] // HEAD
    spans = jnp.stack(
        [
            start,
            base,
            lax.div(begins[0] - base, KB),
            lax.div(start - base + (tok + KB - 1), KB),
            lax.div(begins[-1] - base + (KB - 1), KB),
            lax.div(start - base + 1, KB),
            mine,
        ]
    ).astype(jnp.int32)
    vmem = pl.BlockSpec(memory_space=pltpu.VMEM)
    state = pltpu.VMEM((heads, tok, HEAD), jnp.float32)
    return pl.pallas_call(
        functools.partial(attend_kernel, heads),
        out_shape=jax.ShapeDtypeStruct((tok, heads * HEAD), jnp.bfloat16),
        in_specs=[pl.BlockSpec(memory_space=pltpu.SMEM), vmem, vmem]
        + [pl.BlockSpec(memory_space=pltpu.HBM)] * 4,
        out_specs=vmem,
        scratch_shapes=[
            pltpu.VMEM((2, PLANES, NY, tok, HEAD), jnp.bfloat16),
            state,
            state,
            state,
            pltpu.SemaphoreType.DMA((4, 4)),
        ],
        compiler_params=pltpu.CompilerParams(vmem_limit_bytes=48 * 2**20),
        name="attend",
    )(spans, jnp.broadcast_to(begins[:, None], (tok, HEAD)), queries, *groups)


def per_device(tokens, projection, doc_lengths):
    half = tokens.shape[1]
    tok = 2 * half
    lengths = doc_lengths[0]
    span = HEADS // 2 * HEAD
    mine, plane = lax.axis_index("core"), lax.axis_index("z")
    at_x, at_y = lax.axis_index("x"), lax.axis_index("y")
    own = tokens[0]
    other = swap(own)

    start = ((plane * NY + at_y) * tok).astype(jnp.int32)
    qtok = start + jnp.arange(tok, dtype=jnp.int32)
    begins = doc_begins(lengths, qtok)
    cosine, sine = turn_tables((qtok - begins).astype(jnp.float32))
    place = jnp.stack([mine, at_x, at_y]).astype(jnp.int32)

    small = jnp.stack([projection[:, 2 * span :][:, :HEAD], projection[:, 2 * span + HEAD :]])
    big = jnp.stack([projection[:, :span], projection[:, span : 2 * span]])
    small = along_chips(small)
    small = around(small, "y")
    big = along_chips(big)
    small, big = lax.optimization_barrier((small, big))
    wide = span * 3 // 4
    most, rest = spread(big[..., :wide], "y"), around(big[..., wide:], "x")
    left, right = shift(small, "x", 1), shift(small, "x", -1)
    left, right, cosine, sine, other = lax.optimization_barrier((left, right, cosine, sine, other))
    halves = [shift(left[:2], "x", 1), shift(right[2:], "x", -1)]
    most, rest, halves = lax.optimization_barrier((most, rest, halves))
    small = [small, left, right] + halves
    most = [most] + [shift(most, "x", by) for by in STEPS[1:]]
    rest = [spread(rest, "y")]

    keyed = mine == 0
    tables = jnp.where(keyed, cosine, 1.0), jnp.where(keyed, sine, 0.0)
    keyval = project(place, tables, own, other, [("y, then x", small)], "project_keyval")
    planes = [shift(keyval, "z", PLANES - 1 - p) for p in range(PLANES - 1)] + [keyval]
    near, rest = lax.optimization_barrier((planes[2:], rest))
    late = spread(jnp.stack(near), "y")
    far, most[1], most[2] = lax.optimization_barrier((planes[:2], most[1], most[2]))
    early = spread(jnp.stack(far), "y")
    groups = [early, late, swap(early), swap(late)]

    queries = project(
        place, (cosine, sine), own, other, [("ordered y, then x", most), ("x, then y", rest)], "project_queries"
    )
    base = ((plane - (PLANES - 1)) * (NY * tok)).astype(jnp.int32)
    mixed = attend(queries, groups, begins, start, base, mine).reshape(2, half, span)
    kept = lax.dynamic_index_in_dim(mixed, mine, 0, keepdims=False)
    given = swap(lax.dynamic_index_in_dim(mixed, 1 - mine, 0, keepdims=False))
    return jnp.where(
        keyed, jnp.concatenate([kept, given], axis=1), jnp.concatenate([given, kept], axis=1)
    )[None]


def solution(mesh):
    mesh = Mesh(mesh.devices.reshape(NZ, NY, 2, NX), ("z", "y", "core", "x"))
    everyone = ("z", "y", "core")
    in_specs = (P("x", everyone, None), P(everyone + ("x",), None), P("x", None))
    out_specs = P("x", everyone, None)
    return jax.shard_map(
        per_device, mesh=mesh, in_specs=in_specs, out_specs=out_specs, check_vma=False
    )
```

```python
import functools

import jax
import jax.numpy as jnp
import numpy as np
from jax import lax
from jax.experimental import pallas as pl
from jax.experimental.pallas import tpu as pltpu
from jax.sharding import Mesh
from jax.sharding import PartitionSpec as P

HEADS = 8
HEAD = 128
KB = 1024
LOG2E = 1.4426950408889634
NZ, NY, NX = 8, 4, 4
SIZE = {"z": NZ, "y": NY, "x": NX}
PLANES = 5
STEPS = (0, 1, -1, 2)
CHUNKS = 2


def doc_begins(lengths, tpos):
    ends = jnp.cumsum(lengths)
    after = tpos[:, None] >= ends[None, :]
    return jnp.sum(jnp.where(after, lengths[None, :], 0), axis=1).astype(jnp.int32)


def turn_tables(pos):
    expo = jnp.arange(HEAD // 2).astype(jnp.float32) * (2.0 / HEAD)
    inv = jnp.power(jnp.float32(500000.0), -expo)
    angle = pos[:, None] * inv[None, :]
    cosine, sine = jnp.cos(angle), jnp.sin(angle)
    return (
        jnp.concatenate([cosine, cosine], axis=1),
        jnp.concatenate([-sine, sine], axis=1),
    )


def shift(x, axis, by):
    size = SIZE[axis]
    return lax.ppermute(x, axis, [(i, (i + by) % size) for i in range(size)])


def swap(x):
    return lax.ppermute(x, "core", [(0, 1), (1, 0)])


def along_chips(x):
    wide = jnp.broadcast_to(x[None], (NZ,) + x.shape).reshape((2 * NZ,) + x.shape[1:])
    return lax.all_to_all(wide, ("z", "core"), 0, 0, tiled=True).reshape((NZ,) + x.shape)


def spread(x, axis):
    wide = jnp.broadcast_to(x[None], (SIZE[axis],) + x.shape)
    return lax.all_to_all(wide, axis, 0, 0, tiled=True)


def around(x, axis):
    return jnp.stack([x] + [shift(x, axis, by) for by in STEPS[1:]])


def around_last(x, axis):
    left, right = shift(x, axis, 1), shift(x, axis, -1)
    half = x.shape[0] // 2
    return [x, left, right, shift(left[:half], axis, 1), shift(right[half:], axis, -1)]


def blocks_of(kind, pieces, at_y, at_x):
    if kind == "x, then y":
        return [
            (pieces[0].at[y, j], y, lax.rem(at_x + (8 - STEPS[j]), 4))
            for y in range(NY)
            for j in range(NX)
        ]
    found = []
    for r in range(4):
        for j in range(4):
            if r == 3 and len(pieces) == 3:
                continue
            src = pieces[r].at[j] if r < 3 else pieces[3 + j // 2].at[j % 2]
            y = j if kind == "ordered y, then x" else lax.rem(at_y + (8 - STEPS[j]), 4)
            found.append((src, y, lax.rem(at_x + (8 - STEPS[r]), 4)))
    return found


def turn(sums, cos_ref, sin_ref, out_ref):
    half = HEAD // 2
    for h in range(sums.shape[1] // HEAD):
        vecs = sums[:, h * HEAD : (h + 1) * HEAD]
        turned = jnp.concatenate([vecs[:, half:], vecs[:, :half]], axis=1)
        out_ref[:, h * HEAD : (h + 1) * HEAD] = (
            vecs * cos_ref[...] + turned * sin_ref[...]
        ).astype(jnp.bfloat16)


def pick(rows, x, out_ref):
    lane = lax.broadcasted_iota(jnp.int32, (512, 128), 1)
    source = (lane >> 5) * 128 + x * 32 + (lane & 31)
    one = (lax.broadcasted_iota(jnp.int32, (512, 128), 0) == source).astype(jnp.float32)
    one = one.astype(jnp.bfloat16)
    for y in range(NY):
        for pair in range(NZ // 2):
            slabs = [rows[:, pl.ds((z * NY + y) * 256, 256)] for z in (2 * pair, 2 * pair + 1)]
            picked = jnp.dot(
                jnp.concatenate(slabs, axis=1), one, preferred_element_type=jnp.float32
            )
            column = (y * NZ // 2 + pair) * 128
            out_ref[:, column : column + 128] = picked.astype(jnp.bfloat16)


def project_kernel(kinds, counts, partial, place_ref, cos_ref, sin_ref, own_hbm, other_hbm, *refs):
    jobs = len(kinds)
    pieces = [refs[sum(counts[:job]) : sum(counts[: job + 1])] for job in range(jobs)]
    outs = 2 if partial else 1
    out_refs = refs[sum(counts) : sum(counts) + outs]
    rows, accum, rows_sem, sems, weights = refs[sum(counts) + outs :]
    wides = [piece[0].shape[-1] for piece in pieces]
    mine, at_x, at_y = place_ref[0], place_ref[1], place_ref[2]
    tok = own_hbm.shape[0]
    thick = NZ // CHUNKS
    wide_depth = 256 * NY * thick

    def fetch(chunk):
        planes = pl.ds(chunk * thick, thick)
        deep = pl.ds(chunk * wide_depth, wide_depth)
        copies = []
        for job, kind in enumerate(kinds):
            for n, (src, y, x) in enumerate(blocks_of(kind, pieces[job], at_y, at_x)):
                columns = pl.ds(sum(wides[:job]), wides[job])
                dst = weights.at[planes, y, :, x, :, columns]
                copies.append(pltpu.make_async_copy(src.at[planes], dst, sems.at[chunk, job, n]))
        for k, (src, core) in enumerate(((own_hbm, mine), (other_hbm, 1 - mine))):
            dst = rows.at[pl.ds(pl.multiple_of(core * tok, tok), tok), deep]
            copies.append(pltpu.make_async_copy(src.at[:, deep], dst, rows_sem.at[chunk, k]))
        return copies

    far = lax.rem(at_x + (8 - STEPS[3]), 4)
    if partial:
        empty = jnp.zeros((NZ, NY, 2, 1, 32, wides[0]), jnp.bfloat16)
        weights[:, :, :, pl.ds(far, 1), :, : wides[0]] = empty
    chunks = [fetch(chunk) for chunk in range(CHUNKS)]
    for copies in chunks:
        for copy in copies:
            copy.start()
    accum[...] = jnp.zeros(accum.shape, jnp.float32)
    depth = 256 * NY
    for chunk, copies in enumerate(chunks):
        for copy in copies:
            copy.wait()

        @pl.loop(chunk * thick, (chunk + 1) * thick)
        def _(z):
            left = rows[:, pl.ds(pl.multiple_of(z * depth, depth), depth)]
            right = weights[z].reshape(depth, sum(wides))
            accum[...] += jnp.dot(left, right, preferred_element_type=jnp.float32)

    if partial:
        out_refs[0][...] = accum[...]
        pick(rows, far, out_refs[1])
    else:
        turn(accum[...], cos_ref, sin_ref, out_refs[0])


def project(place, tables, own, other, jobs, name, partial=False):
    tok, depth = own.shape
    wides = [pieces[0].shape[-1] for _, pieces in jobs]
    flat = [piece for _, pieces in jobs for piece in pieces]
    vmem = pl.BlockSpec(memory_space=pltpu.VMEM)
    anywhere = pl.BlockSpec(memory_space=pltpu.HBM)
    outs = jax.ShapeDtypeStruct((2 * tok, sum(wides)), jnp.bfloat16)
    if partial:
        outs = (
            jax.ShapeDtypeStruct((2 * tok, sum(wides)), jnp.float32),
            jax.ShapeDtypeStruct((2 * tok, depth // 4), jnp.bfloat16),
        )
    return pl.pallas_call(
        functools.partial(
            project_kernel, [kind for kind, _ in jobs], [len(pieces) for _, pieces in jobs], partial
        ),
        out_shape=outs,
        in_specs=[pl.BlockSpec(memory_space=pltpu.SMEM), vmem, vmem]
        + [anywhere] * (2 + len(flat)),
        out_specs=jax.tree.map(lambda _: vmem, outs),
        scratch_shapes=[
            pltpu.VMEM((2 * tok, depth), jnp.bfloat16),
            pltpu.VMEM((2 * tok, sum(wides)), jnp.float32),
            pltpu.SemaphoreType.DMA((CHUNKS, 2)),
            pltpu.SemaphoreType.DMA((CHUNKS, len(jobs), 16)),
            pltpu.VMEM((NZ, NY, 2, NX, 32, sum(wides)), jnp.bfloat16),
        ],
        compiler_params=pltpu.CompilerParams(vmem_limit_bytes=58 * 2**20),
        cost_estimate=pl.CostEstimate(
            flops=4 * tok * depth * sum(wides),
            bytes_accessed=2 * depth * (2 * tok + sum(wides)),
            transcendentals=0,
        ),
        name=name,
    )(place, *tables, own, other, *flat)


def finish_kernel(cos_ref, sin_ref, sums_ref, rows_ref, first_ref, second_ref, out_ref):
    deep, wide = first_ref.shape
    more = jnp.dot(rows_ref[:, :deep], first_ref[...], preferred_element_type=jnp.float32)
    more += jnp.dot(rows_ref[:, deep:], second_ref[...], preferred_element_type=jnp.float32)
    sums = jnp.concatenate([sums_ref[:, :wide] + more, sums_ref[:, wide:]], axis=1)
    turn(sums, cos_ref, sin_ref, out_ref)


def finish(tables, sums, rows, pieces):
    vmem = pl.BlockSpec(memory_space=pltpu.VMEM)
    return pl.pallas_call(
        finish_kernel,
        out_shape=jax.ShapeDtypeStruct(sums.shape, jnp.bfloat16),
        in_specs=[vmem] * 6,
        out_specs=vmem,
        compiler_params=pltpu.CompilerParams(vmem_limit_bytes=32 * 2**20),
        name="finish_queries",
    )(*tables, sums, rows, *[piece.reshape(-1, piece.shape[-1]) for piece in pieces])


def attend_kernel(heads, span_ref, begin_ref, q_ref, *refs):
    groups = refs[:4]
    out_ref, kv, top, total, accum, sem = refs[4:]
    start, base, low, high, full_low, full_high, mine = [span_ref[i] for i in range(7)]
    tok = q_ref.shape[0]
    factor = np.float32(HEAD**-0.5 * LOG2E)
    copies = []
    for k, src in enumerate(groups):
        which = mine if k < 2 else 1 - mine
        first = 0 if k % 2 == 0 else PLANES - src.shape[1]
        for r in range(4):
            dst = kv.at[which, pl.ds(first, src.shape[1]), r]
            copies.append(pltpu.make_async_copy(src.at[r], dst, sem.at[k, r]))
    for copy in copies[4:8] + copies[12:] + copies[:4] + copies[8:12]:
        copy.start()

    top[...] = jnp.full(top.shape, -1e30, jnp.float32)
    total[...] = jnp.zeros(total.shape, jnp.float32)
    accum[...] = jnp.zeros(accum.shape, jnp.float32)
    for copy in copies[4:8] + copies[12:]:
        copy.wait()
    parts = KB // tok
    rows = NY // parts
    early = rows * groups[0].shape[1]
    ones = jnp.ones((KB, HEAD), jnp.bfloat16)

    def block(i, masked):
        here = pl.ds(lax.rem(i, rows) * parts, parts)
        keys = kv[0, i // rows, here].reshape(KB, HEAD)
        values = jnp.concatenate([kv[1, i // rows, here].reshape(KB, HEAD), ones], axis=1)
        if masked:
            ktok = lax.broadcasted_iota(jnp.int32, (tok, KB), 1) + (base + i * KB)
            qtok = lax.broadcasted_iota(jnp.int32, (tok, KB), 0) + start
            visible = (ktok >= begin_ref[:, 0:1]) & (ktok <= qtok)

        def score(h):
            return lax.dot_general(
                q_ref[:, h * HEAD : (h + 1) * HEAD],
                keys,
                (((1,), (1,)), ((), ())),
                preferred_element_type=jnp.float32,
            )

        following = score(0)
        for h in range(heads):
            scores = following
            if h + 1 < heads:
                following = score(h + 1)
            if masked:
                scores = jnp.where(visible, scores, -1e30)
            old = top[h]
            new = jnp.maximum(old, jnp.max(scores, axis=1, keepdims=True))
            shrink = jnp.exp2((old - new) * factor)
            weights = jnp.exp2((scores - jnp.tile(new, (1, KB // HEAD))) * factor)
            top[h] = new
            sums = jnp.dot(weights.astype(jnp.bfloat16), values, preferred_element_type=jnp.float32)
            total[h] = total[h] * shrink + sums[:, HEAD:]
            accum[h] = accum[h] * shrink + sums[:, :HEAD]

    def wait_early():
        for copy in copies[:4] + copies[8:12]:
            copy.wait()

    @pl.loop(0, high - low)
    def _(n):
        i = high - 1 - n
        full = (i >= full_low) & (i < full_high)

        @pl.when(i == early - 1)
        def _():
            wait_early()

        @pl.when(full)
        def _():
            block(i, False)

        @pl.when(jnp.logical_not(full))
        def _():
            block(i, True)

    @pl.when(low >= early)
    def _():
        wait_early()

    for h in range(heads):
        out_ref[:, h * HEAD : (h + 1) * HEAD] = (accum[h] / total[h]).astype(jnp.bfloat16)


def attend(queries, groups, begins, start, base, mine):
    tok = queries.shape[0]
    heads = queries.shape[1] // HEAD
    spans = jnp.stack(
        [
            start,
            base,
            lax.div(begins[0] - base, KB),
            lax.div(start - base + (tok + KB - 1), KB),
            lax.div(begins[-1] - base + (KB - 1), KB),
            lax.div(start - base + 1, KB),
            mine,
        ]
    ).astype(jnp.int32)
    vmem = pl.BlockSpec(memory_space=pltpu.VMEM)
    state = pltpu.VMEM((heads, tok, HEAD), jnp.float32)
    return pl.pallas_call(
        functools.partial(attend_kernel, heads),
        out_shape=jax.ShapeDtypeStruct((tok, heads * HEAD), jnp.bfloat16),
        in_specs=[pl.BlockSpec(memory_space=pltpu.SMEM), vmem, vmem]
        + [pl.BlockSpec(memory_space=pltpu.HBM)] * 4,
        out_specs=vmem,
        scratch_shapes=[
            pltpu.VMEM((2, PLANES, NY, tok, HEAD), jnp.bfloat16),
            state,
            state,
            state,
            pltpu.SemaphoreType.DMA((4, 4)),
        ],
        compiler_params=pltpu.CompilerParams(vmem_limit_bytes=48 * 2**20),
        name="attend",
    )(spans, jnp.broadcast_to(begins[:, None], (tok, HEAD)), queries, *groups)


def per_device(tokens, projection, doc_lengths):
    half = tokens.shape[1]
    tok = 2 * half
    lengths = doc_lengths[0]
    span = HEADS // 2 * HEAD
    mine, plane = lax.axis_index("core"), lax.axis_index("z")
    at_x, at_y = lax.axis_index("x"), lax.axis_index("y")
    own = tokens[0]
    other = swap(own)

    start = ((plane * NY + at_y) * tok).astype(jnp.int32)
    qtok = start + jnp.arange(tok, dtype=jnp.int32)
    begins = doc_begins(lengths, qtok)
    cosine, sine = turn_tables((qtok - begins).astype(jnp.float32))
    place = jnp.stack([mine, at_x, at_y]).astype(jnp.int32)

    small = jnp.stack([projection[:, 2 * span :][:, :HEAD], projection[:, 2 * span + HEAD :]])
    big = jnp.stack([projection[:, :span], projection[:, span : 2 * span]])
    small = along_chips(small)
    small = around(small, "y")
    big = along_chips(big)
    small, big = lax.optimization_barrier((small, big))
    wide = span * 3 // 4
    most, rest = spread(big[..., :wide], "y"), around(big[..., wide:], "x")
    left, right = shift(small, "x", 1), shift(small, "x", -1)
    left, right, cosine, sine, other = lax.optimization_barrier((left, right, cosine, sine, other))
    halves = [shift(left[:2], "x", 1), shift(right[2:], "x", -1)]
    most, rest, halves = lax.optimization_barrier((most, rest, halves))
    small = [small, left, right] + halves
    most = [most, shift(most, "x", 1), shift(most, "x", -1)]
    distant = [shift(most[1][:2], "x", 1), shift(most[2][2:], "x", -1)]
    rest = [spread(rest, "y")]

    keyed = mine == 0
    tables = jnp.where(keyed, cosine, 1.0), jnp.where(keyed, sine, 0.0)
    keyval = project(place, tables, own, other, [("y, then x", small)], "project_keyval")
    planes = [shift(keyval, "z", PLANES - 1 - p) for p in range(PLANES - 1)] + [keyval]
    near, rest = lax.optimization_barrier((planes[2:], rest))
    late = spread(jnp.stack(near), "y")
    far, most[1], most[2] = lax.optimization_barrier((planes[:2], most[1], most[2]))
    early = spread(jnp.stack(far), "y")
    jobs = [("ordered y, then x", most), ("x, then y", rest)]
    sums, picked = project(place, (cosine, sine), own, other, jobs, "project_queries", True)
    early, distant, sums = lax.optimization_barrier((early, distant, sums))
    groups = [early, late, swap(early), swap(late)]
    queries = finish((cosine, sine), sums, picked, distant)
    base = ((plane - (PLANES - 1)) * (NY * tok)).astype(jnp.int32)
    mixed = attend(queries, groups, begins, start, base, mine).reshape(2, half, span)
    kept = lax.dynamic_index_in_dim(mixed, mine, 0, keepdims=False)
    given = swap(lax.dynamic_index_in_dim(mixed, 1 - mine, 0, keepdims=False))
    return jnp.where(
        keyed, jnp.concatenate([kept, given], axis=1), jnp.concatenate([given, kept], axis=1)
    )[None]


def solution(mesh):
    mesh = Mesh(mesh.devices.reshape(NZ, NY, 2, NX), ("z", "y", "core", "x"))
    everyone = ("z", "y", "core")
    in_specs = (P("x", everyone, None), P(everyone + ("x",), None), P("x", None))
    out_specs = P("x", everyone, None)
    return jax.shard_map(
        per_device, mesh=mesh, in_specs=in_specs, out_specs=out_specs, check_vma=False
    )
```

```python
import functools

import jax
import jax.numpy as jnp
import numpy as np
from jax import lax
from jax.experimental import pallas as pl
from jax.experimental.pallas import tpu as pltpu
from jax.sharding import Mesh
from jax.sharding import PartitionSpec as P

HEADS = 8
HEAD = 128
KB = 1024
LOG2E = 1.4426950408889634
NZ, NY, NX = 8, 4, 4
SIZE = {"z": NZ, "y": NY, "x": NX}
PLANES, EARLY = 5, 2
STEPS = (0, 1, -1, 2)
CHUNKS = 2


def doc_begins(lengths, tpos):
    ends = jnp.cumsum(lengths)
    after = tpos[:, None] >= ends[None, :]
    return jnp.sum(jnp.where(after, lengths[None, :], 0), axis=1).astype(jnp.int32)


def turn_tables(pos):
    expo = jnp.arange(HEAD // 2).astype(jnp.float32) * (2.0 / HEAD)
    inv = jnp.power(jnp.float32(500000.0), -expo)
    angle = pos[:, None] * inv[None, :]
    cosine, sine = jnp.cos(angle), jnp.sin(angle)
    return (
        jnp.concatenate([cosine, cosine], axis=1),
        jnp.concatenate([-sine, sine], axis=1),
    )


def shift(x, axis, by):
    size = SIZE[axis]
    return lax.ppermute(x, axis, [(i, (i + by) % size) for i in range(size)])


def swap(x):
    return lax.ppermute(x, "core", [(0, 1), (1, 0)])


def along_chips(x):
    wide = jnp.broadcast_to(x[None], (NZ,) + x.shape).reshape((2 * NZ,) + x.shape[1:])
    return lax.all_to_all(wide, ("z", "core"), 0, 0, tiled=True).reshape((NZ,) + x.shape)


def spread(x, axis):
    wide = jnp.broadcast_to(x[None], (SIZE[axis],) + x.shape)
    return lax.all_to_all(wide, axis, 0, 0, tiled=True)


def around(x, axis):
    return jnp.stack([x] + [shift(x, axis, by) for by in STEPS[1:]])


def around_last(x, axis):
    left, right = shift(x, axis, 1), shift(x, axis, -1)
    half = x.shape[0] // 2
    return [x, left, right, shift(left[:half], axis, 1), shift(right[half:], axis, -1)]


def blocks_of(kind, pieces, at_y, at_x):
    if kind == "x, then y":
        return [
            (pieces[0].at[y, j], y, lax.rem(at_x + (8 - STEPS[j]), 4))
            for y in range(NY)
            for j in range(NX)
        ]
    found = []
    for r in range(4):
        for j in range(4):
            if r == 3 and len(pieces) == 3:
                continue
            src = pieces[r].at[j] if r < 3 else pieces[3 + j // 2].at[j % 2]
            y = j if kind == "ordered y, then x" else lax.rem(at_y + (8 - STEPS[j]), 4)
            found.append((src, y, lax.rem(at_x + (8 - STEPS[r]), 4)))
    return found


def turn(sums, cos_ref, sin_ref, out_ref):
    half = HEAD // 2
    for h in range(sums.shape[1] // HEAD):
        vecs = sums[:, h * HEAD : (h + 1) * HEAD]
        turned = jnp.concatenate([vecs[:, half:], vecs[:, :half]], axis=1)
        out_ref[:, h * HEAD : (h + 1) * HEAD] = (
            vecs * cos_ref[...] + turned * sin_ref[...]
        ).astype(jnp.bfloat16)


def pick(rows, x, out_ref):
    lane = lax.broadcasted_iota(jnp.int32, (512, 128), 1)
    source = (lane >> 5) * 128 + x * 32 + (lane & 31)
    one = (lax.broadcasted_iota(jnp.int32, (512, 128), 0) == source).astype(jnp.float32)
    one = one.astype(jnp.bfloat16)
    for y in range(NY):
        for pair in range(NZ // 2):
            slabs = [rows[:, pl.ds((z * NY + y) * 256, 256)] for z in (2 * pair, 2 * pair + 1)]
            picked = jnp.dot(
                jnp.concatenate(slabs, axis=1), one, preferred_element_type=jnp.float32
            )
            column = (y * NZ // 2 + pair) * 128
            out_ref[:, column : column + 128] = picked.astype(jnp.bfloat16)


def project_kernel(kinds, counts, partial, place_ref, cos_ref, sin_ref, own_hbm, other_hbm, *refs):
    jobs = len(kinds)
    pieces = [refs[sum(counts[:job]) : sum(counts[: job + 1])] for job in range(jobs)]
    outs = 2 if partial else 1
    out_refs = refs[sum(counts) : sum(counts) + outs]
    rows, accum, rows_sem, sems, weights = refs[sum(counts) + outs :]
    wides = [piece[0].shape[-1] for piece in pieces]
    mine, at_x, at_y = place_ref[0], place_ref[1], place_ref[2]
    tok = own_hbm.shape[0]
    thick = NZ // CHUNKS
    wide_depth = 256 * NY * thick

    def fetch(chunk):
        planes = pl.ds(chunk * thick, thick)
        deep = pl.ds(chunk * wide_depth, wide_depth)
        copies = []
        for job, kind in enumerate(kinds):
            for n, (src, y, x) in enumerate(blocks_of(kind, pieces[job], at_y, at_x)):
                columns = pl.ds(sum(wides[:job]), wides[job])
                dst = weights.at[planes, y, :, x, :, columns]
                copies.append(pltpu.make_async_copy(src.at[planes], dst, sems.at[chunk, job, n]))
        for k, (src, core) in enumerate(((own_hbm, mine), (other_hbm, 1 - mine))):
            dst = rows.at[pl.ds(pl.multiple_of(core * tok, tok), tok), deep]
            copies.append(pltpu.make_async_copy(src.at[:, deep], dst, rows_sem.at[chunk, k]))
        return copies

    far = lax.rem(at_x + (8 - STEPS[3]), 4)
    if partial:
        empty = jnp.zeros((NZ, NY, 2, 1, 32, wides[0]), jnp.bfloat16)
        weights[:, :, :, pl.ds(far, 1), :, : wides[0]] = empty
    chunks = [fetch(chunk) for chunk in range(CHUNKS)]
    for copies in chunks:
        for copy in copies:
            copy.start()
    accum[...] = jnp.zeros(accum.shape, jnp.float32)
    depth = 256 * NY
    for chunk, copies in enumerate(chunks):
        for copy in copies:
            copy.wait()

        @pl.loop(chunk * thick, (chunk + 1) * thick)
        def _(z):
            left = rows[:, pl.ds(pl.multiple_of(z * depth, depth), depth)]
            right = weights[z].reshape(depth, sum(wides))
            accum[...] += jnp.dot(left, right, preferred_element_type=jnp.float32)

    if partial:
        out_refs[0][...] = accum[...]
        pick(rows, far, out_refs[1])
    else:
        turn(accum[...], cos_ref, sin_ref, out_refs[0])


def project(place, tables, own, other, jobs, name, partial=False):
    tok, depth = own.shape
    wides = [pieces[0].shape[-1] for _, pieces in jobs]
    flat = [piece for _, pieces in jobs for piece in pieces]
    vmem = pl.BlockSpec(memory_space=pltpu.VMEM)
    anywhere = pl.BlockSpec(memory_space=pltpu.HBM)
    outs = jax.ShapeDtypeStruct((2 * tok, sum(wides)), jnp.bfloat16)
    if partial:
        outs = (
            jax.ShapeDtypeStruct((2 * tok, sum(wides)), jnp.float32),
            jax.ShapeDtypeStruct((2 * tok, depth // 4), jnp.bfloat16),
        )
    return pl.pallas_call(
        functools.partial(
            project_kernel, [kind for kind, _ in jobs], [len(pieces) for _, pieces in jobs], partial
        ),
        out_shape=outs,
        in_specs=[pl.BlockSpec(memory_space=pltpu.SMEM), vmem, vmem]
        + [anywhere] * (2 + len(flat)),
        out_specs=jax.tree.map(lambda _: vmem, outs),
        scratch_shapes=[
            pltpu.VMEM((2 * tok, depth), jnp.bfloat16),
            pltpu.VMEM((2 * tok, sum(wides)), jnp.float32),
            pltpu.SemaphoreType.DMA((CHUNKS, 2)),
            pltpu.SemaphoreType.DMA((CHUNKS, len(jobs), 16)),
            pltpu.VMEM((NZ, NY, 2, NX, 32, sum(wides)), jnp.bfloat16),
        ],
        compiler_params=pltpu.CompilerParams(vmem_limit_bytes=58 * 2**20),
        cost_estimate=pl.CostEstimate(
            flops=4 * tok * depth * sum(wides),
            bytes_accessed=2 * depth * (2 * tok + sum(wides)),
            transcendentals=0,
        ),
        name=name,
    )(place, *tables, own, other, *flat)


def finish_kernel(cos_ref, sin_ref, sums_ref, rows_ref, first_ref, second_ref, out_ref):
    deep, wide = first_ref.shape
    more = jnp.dot(rows_ref[:, :deep], first_ref[...], preferred_element_type=jnp.float32)
    more += jnp.dot(rows_ref[:, deep:], second_ref[...], preferred_element_type=jnp.float32)
    sums = jnp.concatenate([sums_ref[:, :wide] + more, sums_ref[:, wide:]], axis=1)
    turn(sums, cos_ref, sin_ref, out_ref)


def finish(tables, sums, rows, pieces):
    vmem = pl.BlockSpec(memory_space=pltpu.VMEM)
    return pl.pallas_call(
        finish_kernel,
        out_shape=jax.ShapeDtypeStruct(sums.shape, jnp.bfloat16),
        in_specs=[vmem] * 6,
        out_specs=vmem,
        compiler_params=pltpu.CompilerParams(vmem_limit_bytes=32 * 2**20),
        name="finish_queries",
    )(*tables, sums, rows, *[piece.reshape(-1, piece.shape[-1]) for piece in pieces])


def attend_kernel(heads, span_ref, begin_ref, q_ref, *refs):
    groups = refs[:2]
    out_ref, kv, top, total, accum, sem = refs[2:]
    start, base, low, high, full_low, full_high, mine = [span_ref[i] for i in range(7)]
    tok = q_ref.shape[0]
    factor = np.float32(HEAD**-0.5 * LOG2E)
    copies = []
    for k in range(4):
        which = mine if k < 2 else 1 - mine
        planes = pl.ds(0, EARLY) if k % 2 == 0 else pl.ds(EARLY, PLANES - EARLY)
        for r in range(4):
            src, dst = groups[k // 2].at[r, planes], kv.at[which, planes, r]
            copies.append(pltpu.make_async_copy(src, dst, sem.at[k, r]))
    for copy in copies[4:8] + copies[12:] + copies[:4] + copies[8:12]:
        copy.start()

    top[...] = jnp.full(top.shape, -1e30, jnp.float32)
    total[...] = jnp.zeros(total.shape, jnp.float32)
    accum[...] = jnp.zeros(accum.shape, jnp.float32)
    for copy in copies[4:8] + copies[12:]:
        copy.wait()
    parts = KB // tok
    rows = NY // parts
    early = rows * EARLY
    ones = jnp.ones((KB, HEAD), jnp.bfloat16)

    def block(i, masked):
        here = pl.ds(lax.rem(i, rows) * parts, parts)
        keys = kv[0, i // rows, here].reshape(KB, HEAD)
        values = jnp.concatenate([kv[1, i // rows, here].reshape(KB, HEAD), ones], axis=1)
        if masked:
            ktok = lax.broadcasted_iota(jnp.int32, (tok, KB), 1) + (base + i * KB)
            qtok = lax.broadcasted_iota(jnp.int32, (tok, KB), 0) + start
            visible = (ktok >= begin_ref[:, 0:1]) & (ktok <= qtok)

        def score(h):
            return lax.dot_general(
                q_ref[:, h * HEAD : (h + 1) * HEAD],
                keys,
                (((1,), (1,)), ((), ())),
                preferred_element_type=jnp.float32,
            )

        following = score(0)
        for h in range(heads):
            scores = following
            if h + 1 < heads:
                following = score(h + 1)
            if masked:
                scores = jnp.where(visible, scores, -1e30)
            old = top[h]
            new = jnp.maximum(old, jnp.max(scores, axis=1, keepdims=True))
            shrink = jnp.exp2((old - new) * factor)
            weights = jnp.exp2((scores - jnp.tile(new, (1, KB // HEAD))) * factor)
            top[h] = new
            sums = jnp.dot(weights.astype(jnp.bfloat16), values, preferred_element_type=jnp.float32)
            total[h] = total[h] * shrink + sums[:, HEAD:]
            accum[h] = accum[h] * shrink + sums[:, :HEAD]

    def wait_early():
        for copy in copies[:4] + copies[8:12]:
            copy.wait()

    @pl.loop(0, high - low)
    def _(n):
        i = high - 1 - n
        full = (i >= full_low) & (i < full_high)

        @pl.when(i == early - 1)
        def _():
            wait_early()

        @pl.when(full)
        def _():
            block(i, False)

        @pl.when(jnp.logical_not(full))
        def _():
            block(i, True)

    @pl.when(low >= early)
    def _():
        wait_early()

    for h in range(heads):
        out_ref[:, h * HEAD : (h + 1) * HEAD] = (accum[h] / total[h]).astype(jnp.bfloat16)


def attend(queries, groups, begins, start, base, mine):
    tok = queries.shape[0]
    heads = queries.shape[1] // HEAD
    spans = jnp.stack(
        [
            start,
            base,
            lax.div(begins[0] - base, KB),
            lax.div(start - base + (tok + KB - 1), KB),
            lax.div(begins[-1] - base + (KB - 1), KB),
            lax.div(start - base + 1, KB),
            mine,
        ]
    ).astype(jnp.int32)
    vmem = pl.BlockSpec(memory_space=pltpu.VMEM)
    state = pltpu.VMEM((heads, tok, HEAD), jnp.float32)
    return pl.pallas_call(
        functools.partial(attend_kernel, heads),
        out_shape=jax.ShapeDtypeStruct((tok, heads * HEAD), jnp.bfloat16),
        in_specs=[pl.BlockSpec(memory_space=pltpu.SMEM), vmem, vmem]
        + [pl.BlockSpec(memory_space=pltpu.HBM)] * 2,
        out_specs=vmem,
        scratch_shapes=[
            pltpu.VMEM((2, PLANES, NY, tok, HEAD), jnp.bfloat16),
            state,
            state,
            state,
            pltpu.SemaphoreType.DMA((4, 4)),
        ],
        compiler_params=pltpu.CompilerParams(vmem_limit_bytes=48 * 2**20),
        name="attend",
    )(spans, jnp.broadcast_to(begins[:, None], (tok, HEAD)), queries, *groups)


def per_device(tokens, projection, doc_lengths):
    half = tokens.shape[1]
    tok = 2 * half
    lengths = doc_lengths[0]
    span = HEADS // 2 * HEAD
    mine, plane = lax.axis_index("core"), lax.axis_index("z")
    at_x, at_y = lax.axis_index("x"), lax.axis_index("y")
    own = tokens[0]
    other = swap(own)

    start = ((plane * NY + at_y) * tok).astype(jnp.int32)
    qtok = start + jnp.arange(tok, dtype=jnp.int32)
    begins = doc_begins(lengths, qtok)
    cosine, sine = turn_tables((qtok - begins).astype(jnp.float32))
    place = jnp.stack([mine, at_x, at_y]).astype(jnp.int32)

    parts = [projection[:, i * span : (i + 1) * span] for i in range(2)]
    ends = [projection[:, 2 * span :][:, :HEAD], projection[:, 2 * span + HEAD :]]
    both = along_chips(jnp.stack([jnp.concatenate(pair, axis=1) for pair in zip(parts, ends)]))
    small, big = around(both[..., span:], "y"), both[..., :span]
    wide = span * 3 // 4
    most, rest = spread(big[..., :wide], "y"), around(big[..., wide:], "x")
    left, right = shift(small, "x", 1), shift(small, "x", -1)
    left, right, cosine, sine, other = lax.optimization_barrier((left, right, cosine, sine, other))
    halves = [shift(left[:2], "x", 1), shift(right[2:], "x", -1)]
    most, rest, halves = lax.optimization_barrier((most, rest, halves))
    small = [small, left, right] + halves
    most = [most, shift(most, "x", 1), shift(most, "x", -1)]
    distant = [shift(most[1][:2], "x", 1), shift(most[2][2:], "x", -1)]
    rest = [spread(rest, "y")]

    keyed = mine == 0
    tables = jnp.where(keyed, cosine, 1.0), jnp.where(keyed, sine, 0.0)
    keyval = project(place, tables, own, other, [("y, then x", small)], "project_keyval")
    planes = [shift(keyval, "z", PLANES - 1 - p) for p in range(PLANES - 1)] + [keyval]
    planes, rest, most[1], most[2] = lax.optimization_barrier((planes, rest, most[1], most[2]))
    keyval = spread(jnp.stack(planes), "y")
    jobs = [("ordered y, then x", most), ("x, then y", rest)]
    sums, picked = project(place, (cosine, sine), own, other, jobs, "project_queries", True)
    keyval, distant, sums = lax.optimization_barrier((keyval, distant, sums))
    groups = [keyval, swap(keyval)]
    queries = finish((cosine, sine), sums, picked, distant)
    base = ((plane - (PLANES - 1)) * (NY * tok)).astype(jnp.int32)
    mixed = attend(queries, groups, begins, start, base, mine).reshape(2, half, span)
    kept = lax.dynamic_index_in_dim(mixed, mine, 0, keepdims=False)
    given = swap(lax.dynamic_index_in_dim(mixed, 1 - mine, 0, keepdims=False))
    return jnp.where(
        keyed, jnp.concatenate([kept, given], axis=1), jnp.concatenate([given, kept], axis=1)
    )[None]


def solution(mesh):
    mesh = Mesh(mesh.devices.reshape(NZ, NY, 2, NX), ("z", "y", "core", "x"))
    everyone = ("z", "y", "core")
    in_specs = (P("x", everyone, None), P(everyone + ("x",), None), P("x", None))
    out_specs = P("x", everyone, None)
    return jax.shard_map(
        per_device, mesh=mesh, in_specs=in_specs, out_specs=out_specs, check_vma=False
    )
```

```python
import functools

import jax
import jax.numpy as jnp
import numpy as np
from jax import lax
from jax.experimental import pallas as pl
from jax.experimental.pallas import tpu as pltpu
from jax.sharding import Mesh
from jax.sharding import PartitionSpec as P

HEADS = 8
HEAD = 128
KB = 1024
LOG2E = 1.4426950408889634
NZ, NY, NX = 8, 4, 4
SIZE = {"z": NZ, "y": NY, "x": NX}
PLANES = 5
STEPS = (0, 1, -1, 2)
CHUNKS = 4


def doc_begins(lengths, tpos):
    ends = jnp.cumsum(lengths)
    after = tpos[:, None] >= ends[None, :]
    return jnp.sum(jnp.where(after, lengths[None, :], 0), axis=1).astype(jnp.int32)


def turn_tables(pos):
    expo = jnp.arange(HEAD // 2).astype(jnp.float32) * (2.0 / HEAD)
    inv = jnp.power(jnp.float32(500000.0), -expo)
    angle = pos[:, None] * inv[None, :]
    cosine, sine = jnp.cos(angle), jnp.sin(angle)
    return (
        jnp.concatenate([cosine, cosine], axis=1),
        jnp.concatenate([-sine, sine], axis=1),
    )


def shift(x, axis, by):
    size = SIZE[axis]
    return lax.ppermute(x, axis, [(i, (i + by) % size) for i in range(size)])


def swap(x):
    return lax.ppermute(x, "core", [(0, 1), (1, 0)])


def along_chips(x):
    wide = jnp.broadcast_to(x[None], (NZ,) + x.shape).reshape((2 * NZ,) + x.shape[1:])
    return lax.all_to_all(wide, ("z", "core"), 0, 0, tiled=True).reshape((NZ,) + x.shape)


def spread(x, axis):
    wide = jnp.broadcast_to(x[None], (SIZE[axis],) + x.shape)
    return lax.all_to_all(wide, axis, 0, 0, tiled=True)


def around(x, axis):
    return jnp.stack([x] + [shift(x, axis, by) for by in STEPS[1:]])


def around_last(x, axis):
    left, right = shift(x, axis, 1), shift(x, axis, -1)
    half = x.shape[0] // 2
    return [x, left, right, shift(left[:half], axis, 1), shift(right[half:], axis, -1)]


def blocks_of(kind, pieces, at_y, at_x):
    if kind == "x, then y":
        return [
            (pieces[0].at[y, j], y, lax.rem(at_x + (8 - STEPS[j]), 4))
            for y in range(NY)
            for j in range(NX)
        ]
    found = []
    for r in range(4):
        for j in range(4):
            if r == 3 and len(pieces) == 3:
                continue
            src = pieces[r].at[j] if r < 3 else pieces[3 + j // 2].at[j % 2]
            y = j if kind == "ordered y, then x" else lax.rem(at_y + (8 - STEPS[j]), 4)
            found.append((src, y, lax.rem(at_x + (8 - STEPS[r]), 4)))
    return found


def turn(sums, cos_ref, sin_ref, out_ref):
    half = HEAD // 2
    for h in range(sums.shape[1] // HEAD):
        vecs = sums[:, h * HEAD : (h + 1) * HEAD]
        turned = jnp.concatenate([vecs[:, half:], vecs[:, :half]], axis=1)
        out_ref[:, h * HEAD : (h + 1) * HEAD] = (
            vecs * cos_ref[...] + turned * sin_ref[...]
        ).astype(jnp.bfloat16)


def pick(rows, x, pairs, out_ref):
    lane = lax.broadcasted_iota(jnp.int32, (512, 128), 1)
    source = (lane >> 5) * 128 + x * 32 + (lane & 31)
    one = (lax.broadcasted_iota(jnp.int32, (512, 128), 0) == source).astype(jnp.float32)
    one = one.astype(jnp.bfloat16)
    for y in range(NY):
        for pair in pairs:
            slabs = [rows[:, pl.ds((z * NY + y) * 256, 256)] for z in (2 * pair, 2 * pair + 1)]
            picked = jnp.dot(
                jnp.concatenate(slabs, axis=1), one, preferred_element_type=jnp.float32
            )
            column = (y * NZ // 2 + pair) * 128
            out_ref[:, column : column + 128] = picked.astype(jnp.bfloat16)


def project_kernel(kinds, counts, partial, place_ref, cos_ref, sin_ref, own_hbm, other_hbm, *refs):
    jobs = len(kinds)
    pieces = [refs[sum(counts[:job]) : sum(counts[: job + 1])] for job in range(jobs)]
    outs = 2 if partial else 1
    out_refs = refs[sum(counts) : sum(counts) + outs]
    rows, accum, rows_sem, sems, weights = refs[sum(counts) + outs :]
    wides = [piece[0].shape[-1] for piece in pieces]
    mine, at_x, at_y = place_ref[0], place_ref[1], place_ref[2]
    tok = own_hbm.shape[0]
    thick = NZ // CHUNKS
    wide_depth = 256 * NY * thick

    def fetch(chunk):
        planes = pl.ds(chunk * thick, thick)
        deep = pl.ds(chunk * wide_depth, wide_depth)
        copies = []
        for job, kind in enumerate(kinds):
            for n, (src, y, x) in enumerate(blocks_of(kind, pieces[job], at_y, at_x)):
                columns = pl.ds(sum(wides[:job]), wides[job])
                dst = weights.at[planes, y, :, x, :, columns]
                copies.append(pltpu.make_async_copy(src.at[planes], dst, sems.at[chunk, job, n]))
        for k, (src, core) in enumerate(((own_hbm, mine), (other_hbm, 1 - mine))):
            dst = rows.at[pl.ds(pl.multiple_of(core * tok, tok), tok), deep]
            copies.append(pltpu.make_async_copy(src.at[:, deep], dst, rows_sem.at[chunk, k]))
        return copies

    far = lax.rem(at_x + (8 - STEPS[3]), 4)
    if partial:
        empty = jnp.zeros((NZ, NY, 2, 1, 32, wides[0]), jnp.bfloat16)
        weights[:, :, :, pl.ds(far, 1), :, : wides[0]] = empty
    chunks = [fetch(chunk) for chunk in range(CHUNKS)]
    for copies in chunks:
        for copy in copies:
            copy.start()
    accum[...] = jnp.zeros(accum.shape, jnp.float32)
    depth = 256 * NY
    for chunk, copies in enumerate(chunks):
        for copy in copies:
            copy.wait()

        @pl.loop(chunk * thick, (chunk + 1) * thick)
        def _(z):
            left = rows[:, pl.ds(pl.multiple_of(z * depth, depth), depth)]
            right = weights[z].reshape(depth, sum(wides))
            accum[...] += jnp.dot(left, right, preferred_element_type=jnp.float32)

        if partial:
            pick(rows, far, range(chunk * thick // 2, (chunk + 1) * thick // 2), out_refs[1])

    if partial:
        out_refs[0][...] = accum[...]
    else:
        turn(accum[...], cos_ref, sin_ref, out_refs[0])


def project(place, tables, own, other, jobs, name, partial=False):
    tok, depth = own.shape
    wides = [pieces[0].shape[-1] for _, pieces in jobs]
    flat = [piece for _, pieces in jobs for piece in pieces]
    vmem = pl.BlockSpec(memory_space=pltpu.VMEM)
    anywhere = pl.BlockSpec(memory_space=pltpu.HBM)
    outs = jax.ShapeDtypeStruct((2 * tok, sum(wides)), jnp.bfloat16)
    if partial:
        outs = (
            jax.ShapeDtypeStruct((2 * tok, sum(wides)), jnp.float32),
            jax.ShapeDtypeStruct((2 * tok, depth // 4), jnp.bfloat16),
        )
    return pl.pallas_call(
        functools.partial(
            project_kernel, [kind for kind, _ in jobs], [len(pieces) for _, pieces in jobs], partial
        ),
        out_shape=outs,
        in_specs=[pl.BlockSpec(memory_space=pltpu.SMEM), vmem, vmem]
        + [anywhere] * (2 + len(flat)),
        out_specs=jax.tree.map(lambda _: vmem, outs),
        scratch_shapes=[
            pltpu.VMEM((2 * tok, depth), jnp.bfloat16),
            pltpu.VMEM((2 * tok, sum(wides)), jnp.float32),
            pltpu.SemaphoreType.DMA((CHUNKS, 2)),
            pltpu.SemaphoreType.DMA((CHUNKS, len(jobs), 16)),
            pltpu.VMEM((NZ, NY, 2, NX, 32, sum(wides)), jnp.bfloat16),
        ],
        compiler_params=pltpu.CompilerParams(vmem_limit_bytes=48 * 2**20),
        cost_estimate=pl.CostEstimate(
            flops=4 * tok * depth * sum(wides),
            bytes_accessed=2 * depth * (2 * tok + sum(wides)),
            transcendentals=0,
        ),
        name=name,
    )(place, *tables, own, other, *flat)


def finish_kernel(cos_ref, sin_ref, sums_ref, rows_ref, first_ref, second_ref, out_ref):
    deep, wide = first_ref.shape
    more = jnp.dot(rows_ref[:, :deep], first_ref[...], preferred_element_type=jnp.float32)
    more += jnp.dot(rows_ref[:, deep:], second_ref[...], preferred_element_type=jnp.float32)
    sums = jnp.concatenate([sums_ref[:, :wide] + more, sums_ref[:, wide:]], axis=1)
    turn(sums, cos_ref, sin_ref, out_ref)


def finish(tables, sums, rows, pieces):
    vmem = pl.BlockSpec(memory_space=pltpu.VMEM)
    return pl.pallas_call(
        finish_kernel,
        out_shape=jax.ShapeDtypeStruct(sums.shape, jnp.bfloat16),
        in_specs=[vmem] * 6,
        out_specs=vmem,
        compiler_params=pltpu.CompilerParams(vmem_limit_bytes=32 * 2**20),
        name="finish_queries",
    )(*tables, sums, rows, *[piece.reshape(-1, piece.shape[-1]) for piece in pieces])


def attend_kernel(heads, span_ref, begin_ref, q_ref, *refs):
    groups = refs[:4]
    out_ref, kv, top, total, accum, sem = refs[4:]
    start, base, low, high, full_low, full_high, mine = [span_ref[i] for i in range(7)]
    tok = q_ref.shape[0]
    factor = np.float32(HEAD**-0.5 * LOG2E)
    copies = []
    for k, src in enumerate(groups):
        which = mine if k < 2 else 1 - mine
        first = 0 if k % 2 == 0 else PLANES - src.shape[1]
        for r in range(4):
            dst = kv.at[which, pl.ds(first, src.shape[1]), r]
            copies.append(pltpu.make_async_copy(src.at[r], dst, sem.at[k, r]))
    for copy in copies[4:8] + copies[12:] + copies[:4] + copies[8:12]:
        copy.start()

    top[...] = jnp.full(top.shape, -1e30, jnp.float32)
    total[...] = jnp.zeros(total.shape, jnp.float32)
    accum[...] = jnp.zeros(accum.shape, jnp.float32)
    for copy in copies[4:8] + copies[12:]:
        copy.wait()
    parts = KB // tok
    rows = NY // parts
    early = rows * groups[0].shape[1]
    ones = jnp.ones((KB, HEAD), jnp.bfloat16)

    def block(i, masked):
        here = pl.ds(lax.rem(i, rows) * parts, parts)
        keys = kv[0, i // rows, here].reshape(KB, HEAD)
        values = jnp.concatenate([kv[1, i // rows, here].reshape(KB, HEAD), ones], axis=1)
        if masked:
            ktok = lax.broadcasted_iota(jnp.int32, (tok, KB), 1) + (base + i * KB)
            qtok = lax.broadcasted_iota(jnp.int32, (tok, KB), 0) + start
            visible = (ktok >= begin_ref[:, 0:1]) & (ktok <= qtok)

        def score(h):
            return lax.dot_general(
                q_ref[:, h * HEAD : (h + 1) * HEAD],
                keys,
                (((1,), (1,)), ((), ())),
                preferred_element_type=jnp.float32,
            )

        following = score(0)
        for h in range(heads):
            scores = following
            if h + 1 < heads:
                following = score(h + 1)
            if masked:
                scores = jnp.where(visible, scores, -1e30)
            old = top[h]
            new = jnp.maximum(old, jnp.max(scores, axis=1, keepdims=True))
            shrink = jnp.exp2((old - new) * factor)
            weights = jnp.exp2((scores - jnp.tile(new, (1, KB // HEAD))) * factor)
            top[h] = new
            sums = jnp.dot(weights.astype(jnp.bfloat16), values, preferred_element_type=jnp.float32)
            total[h] = total[h] * shrink + sums[:, HEAD:]
            accum[h] = accum[h] * shrink + sums[:, :HEAD]

    def wait_early():
        for copy in copies[:4] + copies[8:12]:
            copy.wait()

    @pl.loop(0, high - low)
    def _(n):
        i = high - 1 - n
        full = (i >= full_low) & (i < full_high)

        @pl.when(i == early - 1)
        def _():
            wait_early()

        @pl.when(full)
        def _():
            block(i, False)

        @pl.when(jnp.logical_not(full))
        def _():
            block(i, True)

    @pl.when(low >= early)
    def _():
        wait_early()

    for h in range(heads):
        out_ref[:, h * HEAD : (h + 1) * HEAD] = (accum[h] / total[h]).astype(jnp.bfloat16)


def attend(queries, groups, begins, start, base, mine):
    tok = queries.shape[0]
    heads = queries.shape[1] // HEAD
    spans = jnp.stack(
        [
            start,
            base,
            lax.div(begins[0] - base, KB),
            lax.div(start - base + (tok + KB - 1), KB),
            lax.div(begins[-1] - base + (KB - 1), KB),
            lax.div(start - base + 1, KB),
            mine,
        ]
    ).astype(jnp.int32)
    vmem = pl.BlockSpec(memory_space=pltpu.VMEM)
    state = pltpu.VMEM((heads, tok, HEAD), jnp.float32)
    return pl.pallas_call(
        functools.partial(attend_kernel, heads),
        out_shape=jax.ShapeDtypeStruct((tok, heads * HEAD), jnp.bfloat16),
        in_specs=[pl.BlockSpec(memory_space=pltpu.SMEM), vmem, vmem]
        + [pl.BlockSpec(memory_space=pltpu.HBM)] * 4,
        out_specs=vmem,
        scratch_shapes=[
            pltpu.VMEM((2, PLANES, NY, tok, HEAD), jnp.bfloat16),
            state,
            state,
            state,
            pltpu.SemaphoreType.DMA((4, 4)),
        ],
        compiler_params=pltpu.CompilerParams(vmem_limit_bytes=48 * 2**20),
        name="attend",
    )(spans, jnp.broadcast_to(begins[:, None], (tok, HEAD)), queries, *groups)


def per_device(tokens, projection, doc_lengths):
    half = tokens.shape[1]
    tok = 2 * half
    lengths = doc_lengths[0]
    span = HEADS // 2 * HEAD
    mine, plane = lax.axis_index("core"), lax.axis_index("z")
    at_x, at_y = lax.axis_index("x"), lax.axis_index("y")
    own = tokens[0]
    other = swap(own)

    start = ((plane * NY + at_y) * tok).astype(jnp.int32)
    qtok = start + jnp.arange(tok, dtype=jnp.int32)
    begins = doc_begins(lengths, qtok)
    cosine, sine = turn_tables((qtok - begins).astype(jnp.float32))
    place = jnp.stack([mine, at_x, at_y]).astype(jnp.int32)

    small = jnp.stack([projection[:, 2 * span :][:, :HEAD], projection[:, 2 * span + HEAD :]])
    big = jnp.stack([projection[:, :span], projection[:, span : 2 * span]])
    small = along_chips(small)
    small = around(small, "y")
    big = along_chips(big)
    small, big = lax.optimization_barrier((small, big))
    wide = span * 3 // 4
    most, rest = spread(big[..., :wide], "y"), around(big[..., wide:], "x")
    left, right = shift(small, "x", 1), shift(small, "x", -1)
    left, right, cosine, sine, other = lax.optimization_barrier((left, right, cosine, sine, other))
    halves = [shift(left[:2], "x", 1), shift(right[2:], "x", -1)]
    most, rest, halves = lax.optimization_barrier((most, rest, halves))
    small = [small, left, right] + halves
    most = [most, shift(most, "x", 1), shift(most, "x", -1)]
    distant = [shift(most[1][:2], "x", 1), shift(most[2][2:], "x", -1)]
    rest = [spread(rest, "y")]

    keyed = mine == 0
    tables = jnp.where(keyed, cosine, 1.0), jnp.where(keyed, sine, 0.0)
    keyval = project(place, tables, own, other, [("y, then x", small)], "project_keyval")
    planes = [shift(keyval, "z", PLANES - 1 - p) for p in range(PLANES - 1)] + [keyval]
    near, rest = lax.optimization_barrier((planes[2:], rest))
    late = spread(jnp.stack(near), "y")
    far, most[1], most[2] = lax.optimization_barrier((planes[:2], most[1], most[2]))
    early = spread(jnp.stack(far), "y")
    jobs = [("ordered y, then x", most), ("x, then y", rest)]
    sums, picked = project(place, (cosine, sine), own, other, jobs, "project_queries", True)
    early, distant, sums = lax.optimization_barrier((early, distant, sums))
    groups = [early, late, swap(early), swap(late)]
    queries = finish((cosine, sine), sums, picked, distant)
    base = ((plane - (PLANES - 1)) * (NY * tok)).astype(jnp.int32)
    mixed = attend(queries, groups, begins, start, base, mine).reshape(2, half, span)
    kept = lax.dynamic_index_in_dim(mixed, mine, 0, keepdims=False)
    given = swap(lax.dynamic_index_in_dim(mixed, 1 - mine, 0, keepdims=False))
    return jnp.where(
        keyed, jnp.concatenate([kept, given], axis=1), jnp.concatenate([given, kept], axis=1)
    )[None]


def solution(mesh):
    mesh = Mesh(mesh.devices.reshape(NZ, NY, 2, NX), ("z", "y", "core", "x"))
    everyone = ("z", "y", "core")
    in_specs = (P("x", everyone, None), P(everyone + ("x",), None), P("x", None))
    out_specs = P("x", everyone, None)
    return jax.shard_map(
        per_device, mesh=mesh, in_specs=in_specs, out_specs=out_specs, check_vma=False
    )
```

```python
import functools

import jax
import jax.numpy as jnp
import numpy as np
from jax import lax
from jax.experimental import pallas as pl
from jax.experimental.pallas import tpu as pltpu
from jax.sharding import Mesh
from jax.sharding import PartitionSpec as P

HEADS = 8
HEAD = 128
KB = 1024
LOG2E = 1.4426950408889634
NZ, NY, NX = 8, 4, 4
SIZE = {"z": NZ, "y": NY, "x": NX}
PLANES = 5
STEPS = (0, 1, -1, 2)
CHUNKS = 4


def doc_begins(lengths, tpos):
    ends = jnp.cumsum(lengths)
    after = tpos[:, None] >= ends[None, :]
    return jnp.sum(jnp.where(after, lengths[None, :], 0), axis=1).astype(jnp.int32)


def turn_tables(pos):
    expo = jnp.arange(HEAD // 2).astype(jnp.float32) * (2.0 / HEAD)
    inv = jnp.power(jnp.float32(500000.0), -expo)
    angle = pos[:, None] * inv[None, :]
    cosine, sine = jnp.cos(angle), jnp.sin(angle)
    return (
        jnp.concatenate([cosine, cosine], axis=1),
        jnp.concatenate([-sine, sine], axis=1),
    )


def shift(x, axis, by):
    size = SIZE[axis]
    return lax.ppermute(x, axis, [(i, (i + by) % size) for i in range(size)])


def swap(x):
    return lax.ppermute(x, "core", [(0, 1), (1, 0)])


def along_chips(x):
    wide = jnp.broadcast_to(x[None], (NZ,) + x.shape).reshape((2 * NZ,) + x.shape[1:])
    return lax.all_to_all(wide, ("z", "core"), 0, 0, tiled=True).reshape((NZ,) + x.shape)


def spread(x, axis):
    wide = jnp.broadcast_to(x[None], (SIZE[axis],) + x.shape)
    return lax.all_to_all(wide, axis, 0, 0, tiled=True)


def around(x, axis):
    return jnp.stack([x] + [shift(x, axis, by) for by in STEPS[1:]])


def around_last(x, axis):
    left, right = shift(x, axis, 1), shift(x, axis, -1)
    half = x.shape[0] // 2
    return [x, left, right, shift(left[:half], axis, 1), shift(right[half:], axis, -1)]


def blocks_of(kind, pieces, at_y, at_x):
    if kind == "x, then y":
        return [
            (pieces[0].at[y, j], y, lax.rem(at_x + (8 - STEPS[j]), 4))
            for y in range(NY)
            for j in range(NX)
        ]
    found = []
    for r in range(4):
        for j in range(4):
            if r == 3 and len(pieces) == 3:
                continue
            src = pieces[r].at[j] if r < 3 else pieces[3 + j // 2].at[j % 2]
            y = j if kind == "ordered y, then x" else lax.rem(at_y + (8 - STEPS[j]), 4)
            found.append((src, y, lax.rem(at_x + (8 - STEPS[r]), 4)))
    return found


def turn(sums, cos_ref, sin_ref, out_ref):
    half = HEAD // 2
    for h in range(sums.shape[1] // HEAD):
        vecs = sums[:, h * HEAD : (h + 1) * HEAD]
        turned = jnp.concatenate([vecs[:, half:], vecs[:, :half]], axis=1)
        out_ref[:, h * HEAD : (h + 1) * HEAD] = (
            vecs * cos_ref[...] + turned * sin_ref[...]
        ).astype(jnp.bfloat16)


def pick(rows, x, pairs, out_ref):
    lane = lax.broadcasted_iota(jnp.int32, (512, 128), 1)
    source = (lane >> 5) * 128 + x * 32 + (lane & 31)
    one = (lax.broadcasted_iota(jnp.int32, (512, 128), 0) == source).astype(jnp.float32)
    one = one.astype(jnp.bfloat16)
    for y in range(NY):
        for pair in pairs:
            slabs = [rows[:, pl.ds((z * NY + y) * 256, 256)] for z in (2 * pair, 2 * pair + 1)]
            picked = jnp.dot(
                jnp.concatenate(slabs, axis=1), one, preferred_element_type=jnp.float32
            )
            column = (y * NZ // 2 + pair) * 128
            out_ref[:, column : column + 128] = picked.astype(jnp.bfloat16)


def project_kernel(kinds, counts, partial, place_ref, cos_ref, sin_ref, own_hbm, other_hbm, *refs):
    jobs = len(kinds)
    pieces = [refs[sum(counts[:job]) : sum(counts[: job + 1])] for job in range(jobs)]
    outs = 2 if partial else 1
    out_refs = refs[sum(counts) : sum(counts) + outs]
    rows, accum, rows_sem, sems, weights = refs[sum(counts) + outs :]
    wides = [piece[0].shape[-1] for piece in pieces]
    mine, at_x, at_y = place_ref[0], place_ref[1], place_ref[2]
    tok = own_hbm.shape[0]
    thick = NZ // CHUNKS
    wide_depth = 256 * NY * thick

    def fetch(chunk):
        planes = pl.ds(chunk * thick, thick)
        deep = pl.ds(chunk * wide_depth, wide_depth)
        copies = []
        for job, kind in enumerate(kinds):
            for n, (src, y, x) in enumerate(blocks_of(kind, pieces[job], at_y, at_x)):
                columns = pl.ds(sum(wides[:job]), wides[job])
                dst = weights.at[planes, y, :, x, :, columns]
                copies.append(pltpu.make_async_copy(src.at[planes], dst, sems.at[chunk, job, n]))
        for k, (src, core) in enumerate(((own_hbm, mine), (other_hbm, 1 - mine))):
            dst = rows.at[pl.ds(pl.multiple_of(core * tok, tok), tok), deep]
            copies.append(pltpu.make_async_copy(src.at[:, deep], dst, rows_sem.at[chunk, k]))
        return copies

    far = lax.rem(at_x + (8 - STEPS[3]), 4)
    if partial:
        empty = jnp.zeros((NZ, NY, 2, 1, 32, wides[0]), jnp.bfloat16)
        weights[:, :, :, pl.ds(far, 1), :, : wides[0]] = empty
    chunks = [fetch(chunk) for chunk in range(CHUNKS)]
    for copies in chunks:
        for copy in copies:
            copy.start()
    accum[...] = jnp.zeros(accum.shape, jnp.float32)
    depth = 256 * NY
    for chunk, copies in enumerate(chunks):
        for copy in copies:
            copy.wait()

        @pl.loop(chunk * thick, (chunk + 1) * thick)
        def _(z):
            left = rows[:, pl.ds(pl.multiple_of(z * depth, depth), depth)]
            right = weights[z].reshape(depth, sum(wides))
            accum[...] += jnp.dot(left, right, preferred_element_type=jnp.float32)

        if partial:
            pick(rows, far, range(chunk * thick // 2, (chunk + 1) * thick // 2), out_refs[1])

    if partial:
        out_refs[0][...] = accum[...]
    else:
        turn(accum[...], cos_ref, sin_ref, out_refs[0])


def project(place, tables, own, other, jobs, name, partial=False):
    tok, depth = own.shape
    wides = [pieces[0].shape[-1] for _, pieces in jobs]
    flat = [piece for _, pieces in jobs for piece in pieces]
    vmem = pl.BlockSpec(memory_space=pltpu.VMEM)
    anywhere = pl.BlockSpec(memory_space=pltpu.HBM)
    outs = jax.ShapeDtypeStruct((2 * tok, sum(wides)), jnp.bfloat16)
    if partial:
        outs = (
            jax.ShapeDtypeStruct((2 * tok, sum(wides)), jnp.float32),
            jax.ShapeDtypeStruct((2 * tok, depth // 4), jnp.bfloat16),
        )
    return pl.pallas_call(
        functools.partial(
            project_kernel, [kind for kind, _ in jobs], [len(pieces) for _, pieces in jobs], partial
        ),
        out_shape=outs,
        in_specs=[pl.BlockSpec(memory_space=pltpu.SMEM), vmem, vmem]
        + [anywhere] * (2 + len(flat)),
        out_specs=jax.tree.map(lambda _: vmem, outs),
        scratch_shapes=[
            pltpu.VMEM((2 * tok, depth), jnp.bfloat16),
            pltpu.VMEM((2 * tok, sum(wides)), jnp.float32),
            pltpu.SemaphoreType.DMA((CHUNKS, 2)),
            pltpu.SemaphoreType.DMA((CHUNKS, len(jobs), 16)),
            pltpu.VMEM((NZ, NY, 2, NX, 32, sum(wides)), jnp.bfloat16),
        ],
        compiler_params=pltpu.CompilerParams(vmem_limit_bytes=48 * 2**20),
        cost_estimate=pl.CostEstimate(
            flops=4 * tok * depth * sum(wides),
            bytes_accessed=2 * depth * (2 * tok + sum(wides)),
            transcendentals=0,
        ),
        name=name,
    )(place, *tables, own, other, *flat)


def finish_kernel(cos_ref, sin_ref, sums_ref, rows_ref, first_ref, second_ref, out_ref):
    deep, wide = first_ref.shape
    more = jnp.dot(rows_ref[:, :deep], first_ref[...], preferred_element_type=jnp.float32)
    more += jnp.dot(rows_ref[:, deep:], second_ref[...], preferred_element_type=jnp.float32)
    sums = jnp.concatenate([sums_ref[:, :wide] + more, sums_ref[:, wide:]], axis=1)
    turn(sums, cos_ref, sin_ref, out_ref)


def finish(tables, sums, rows, pieces):
    vmem = pl.BlockSpec(memory_space=pltpu.VMEM)
    return pl.pallas_call(
        finish_kernel,
        out_shape=jax.ShapeDtypeStruct(sums.shape, jnp.bfloat16),
        in_specs=[vmem] * 6,
        out_specs=vmem,
        compiler_params=pltpu.CompilerParams(vmem_limit_bytes=32 * 2**20),
        name="finish_queries",
    )(*tables, sums, rows, *[piece.reshape(-1, piece.shape[-1]) for piece in pieces])


def attend_kernel(heads, span_ref, begin_ref, q_ref, *refs):
    groups = refs[:4]
    out_ref, kv, top, total, accum, sem = refs[4:]
    start, base, low, high, full_low, full_high, mine = [span_ref[i] for i in range(7)]
    tok = q_ref.shape[0]
    factor = np.float32(HEAD**-0.5 * LOG2E)
    copies = []
    for k, src in enumerate(groups):
        which = mine if k < 2 else 1 - mine
        first = 0 if k % 2 == 0 else PLANES - src.shape[1]
        for r in range(4):
            dst = kv.at[which, pl.ds(first, src.shape[1]), r]
            copies.append(pltpu.make_async_copy(src.at[r], dst, sem.at[k, r]))
    for copy in copies[4:8] + copies[12:] + copies[:4] + copies[8:12]:
        copy.start()

    top[...] = jnp.full(top.shape, -1e30, jnp.float32)
    total[...] = jnp.zeros(total.shape, jnp.float32)
    accum[...] = jnp.zeros(accum.shape, jnp.float32)
    for copy in copies[4:8] + copies[12:]:
        copy.wait()
    parts = KB // tok
    rows = NY // parts
    early = rows * groups[0].shape[1]
    ones = jnp.ones((KB, HEAD), jnp.bfloat16)

    def block(i, masked):
        here = pl.ds(lax.rem(i, rows) * parts, parts)
        keys = kv[0, i // rows, here].reshape(KB, HEAD)
        values = jnp.concatenate([kv[1, i // rows, here].reshape(KB, HEAD), ones], axis=1)
        if masked:
            ktok = lax.broadcasted_iota(jnp.int32, (tok, KB), 1) + (base + i * KB)
            qtok = lax.broadcasted_iota(jnp.int32, (tok, KB), 0) + start
            visible = (ktok >= begin_ref[:, 0:1]) & (ktok <= qtok)

        def score(h):
            return lax.dot_general(
                q_ref[:, h * HEAD : (h + 1) * HEAD],
                keys,
                (((1,), (1,)), ((), ())),
                preferred_element_type=jnp.float32,
            )

        following = score(0)
        for h in range(heads):
            scores = following
            if h + 1 < heads:
                following = score(h + 1)
            if masked:
                scores = jnp.where(visible, scores, -1e30)
            old = top[h]
            new = jnp.maximum(old, jnp.max(scores, axis=1, keepdims=True))
            shrink = jnp.exp2((old - new) * factor)
            weights = jnp.exp2((scores - jnp.tile(new, (1, KB // HEAD))) * factor)
            top[h] = new
            sums = jnp.dot(weights.astype(jnp.bfloat16), values, preferred_element_type=jnp.float32)
            total[h] = total[h] * shrink + sums[:, HEAD:]
            accum[h] = accum[h] * shrink + sums[:, :HEAD]

    def wait_early():
        for copy in copies[:4] + copies[8:12]:
            copy.wait()

    @pl.loop(0, high - low)
    def _(n):
        i = high - 1 - n
        full = (i >= full_low) & (i < full_high)

        @pl.when(i == early - 1)
        def _():
            wait_early()

        @pl.when(full)
        def _():
            block(i, False)

        @pl.when(jnp.logical_not(full))
        def _():
            block(i, True)

    @pl.when(low >= early)
    def _():
        wait_early()

    for h in range(heads):
        out_ref[:, h * HEAD : (h + 1) * HEAD] = (accum[h] / total[h]).astype(jnp.bfloat16)


def attend(queries, groups, begins, start, base, mine):
    tok = queries.shape[0]
    heads = queries.shape[1] // HEAD
    spans = jnp.stack(
        [
            start,
            base,
            lax.div(begins[0] - base, KB),
            lax.div(start - base + (tok + KB - 1), KB),
            lax.div(begins[-1] - base + (KB - 1), KB),
            lax.div(start - base + 1, KB),
            mine,
        ]
    ).astype(jnp.int32)
    vmem = pl.BlockSpec(memory_space=pltpu.VMEM)
    state = pltpu.VMEM((heads, tok, HEAD), jnp.float32)
    return pl.pallas_call(
        functools.partial(attend_kernel, heads),
        out_shape=jax.ShapeDtypeStruct((tok, heads * HEAD), jnp.bfloat16),
        in_specs=[pl.BlockSpec(memory_space=pltpu.SMEM), vmem, vmem]
        + [pl.BlockSpec(memory_space=pltpu.HBM)] * 4,
        out_specs=vmem,
        scratch_shapes=[
            pltpu.VMEM((2, PLANES, NY, tok, HEAD), jnp.bfloat16),
            state,
            state,
            state,
            pltpu.SemaphoreType.DMA((4, 4)),
        ],
        compiler_params=pltpu.CompilerParams(vmem_limit_bytes=48 * 2**20),
        name="attend",
    )(spans, jnp.broadcast_to(begins[:, None], (tok, HEAD)), queries, *groups)


def per_device(tokens, projection, doc_lengths):
    half = tokens.shape[1]
    tok = 2 * half
    lengths = doc_lengths[0]
    span = HEADS // 2 * HEAD
    mine, plane = lax.axis_index("core"), lax.axis_index("z")
    at_x, at_y = lax.axis_index("x"), lax.axis_index("y")
    own = tokens[0]
    other = swap(own)

    start = ((plane * NY + at_y) * tok).astype(jnp.int32)
    qtok = start + jnp.arange(tok, dtype=jnp.int32)
    begins = doc_begins(lengths, qtok)
    cosine, sine = turn_tables((qtok - begins).astype(jnp.float32))
    place = jnp.stack([mine, at_x, at_y]).astype(jnp.int32)

    small = jnp.stack([projection[:, 2 * span :][:, :HEAD], projection[:, 2 * span + HEAD :]])
    big = jnp.stack([projection[:, :span], projection[:, span : 2 * span]])
    small = along_chips(small)
    small = around(small, "y")
    big = along_chips(big)
    small, big = lax.optimization_barrier((small, big))
    wide = span * 3 // 4
    most, rest = spread(big[..., :wide], "y"), around(big[..., wide:], "x")
    left, right = shift(small, "x", 1), shift(small, "x", -1)
    left, right, cosine, sine, other = lax.optimization_barrier((left, right, cosine, sine, other))
    halves = [shift(left[:2], "x", 1), shift(right[2:], "x", -1)]
    most, rest, halves = lax.optimization_barrier((most, rest, halves))
    small = [small, left, right] + halves
    most = [most, shift(most, "x", 1), shift(most, "x", -1)]
    distant = [shift(most[1][:2], "x", 1), shift(most[2][2:], "x", -1)]
    rest = [spread(rest, "y")]

    keyed = mine == 0
    tables = jnp.where(keyed, cosine, 1.0), jnp.where(keyed, sine, 0.0)
    keyval = project(place, tables, own, other, [("y, then x", small)], "project_keyval")
    near = [shift(keyval, "z", 2), shift(keyval, "z", 1)]
    far = shift(jnp.stack(near), "z", 2)
    near, rest = lax.optimization_barrier((near + [keyval], rest))
    late = spread(jnp.stack(near), "y")
    far, most[1], most[2] = lax.optimization_barrier((far, most[1], most[2]))
    early = spread(far, "y")
    jobs = [("ordered y, then x", most), ("x, then y", rest)]
    sums, picked = project(place, (cosine, sine), own, other, jobs, "project_queries", True)
    early, distant, sums = lax.optimization_barrier((early, distant, sums))
    groups = [early, late, swap(early), swap(late)]
    queries = finish((cosine, sine), sums, picked, distant)
    base = ((plane - (PLANES - 1)) * (NY * tok)).astype(jnp.int32)
    mixed = attend(queries, groups, begins, start, base, mine).reshape(2, half, span)
    kept = lax.dynamic_index_in_dim(mixed, mine, 0, keepdims=False)
    given = swap(lax.dynamic_index_in_dim(mixed, 1 - mine, 0, keepdims=False))
    return jnp.where(
        keyed, jnp.concatenate([kept, given], axis=1), jnp.concatenate([given, kept], axis=1)
    )[None]


def solution(mesh):
    mesh = Mesh(mesh.devices.reshape(NZ, NY, 2, NX), ("z", "y", "core", "x"))
    everyone = ("z", "y", "core")
    in_specs = (P("x", everyone, None), P(everyone + ("x",), None), P("x", None))
    out_specs = P("x", everyone, None)
    return jax.shard_map(
        per_device, mesh=mesh, in_specs=in_specs, out_specs=out_specs, check_vma=False
    )
```

```python
import functools

import jax
import jax.numpy as jnp
import numpy as np
from jax import lax
from jax.experimental import pallas as pl
from jax.experimental.pallas import tpu as pltpu
from jax.sharding import Mesh
from jax.sharding import PartitionSpec as P

HEADS = 8
HEAD = 128
KB = 1024
LOG2E = 1.4426950408889634
NZ, NY, NX = 8, 4, 4
SIZE = {"z": NZ, "y": NY, "x": NX}
PLANES = 5
STEPS = (0, 1, -1, 2)
CHUNKS = 4


def doc_begins(lengths, tpos):
    ends = jnp.cumsum(lengths)
    after = tpos[:, None] >= ends[None, :]
    return jnp.sum(jnp.where(after, lengths[None, :], 0), axis=1).astype(jnp.int32)


def turn_tables(pos):
    expo = jnp.arange(HEAD // 2).astype(jnp.float32) * (2.0 / HEAD)
    inv = jnp.power(jnp.float32(500000.0), -expo)
    angle = pos[:, None] * inv[None, :]
    cosine, sine = jnp.cos(angle), jnp.sin(angle)
    return (
        jnp.concatenate([cosine, cosine], axis=1),
        jnp.concatenate([-sine, sine], axis=1),
    )


def shift(x, axis, by):
    size = SIZE[axis]
    return lax.ppermute(x, axis, [(i, (i + by) % size) for i in range(size)])


def swap(x):
    return lax.ppermute(x, "core", [(0, 1), (1, 0)])


def along_chips(x):
    wide = jnp.broadcast_to(x[None], (NZ,) + x.shape).reshape((2 * NZ,) + x.shape[1:])
    return lax.all_to_all(wide, ("z", "core"), 0, 0, tiled=True).reshape((NZ,) + x.shape)


def spread(x, axis):
    wide = jnp.broadcast_to(x[None], (SIZE[axis],) + x.shape)
    return lax.all_to_all(wide, axis, 0, 0, tiled=True)


def around(x, axis):
    return jnp.stack([x] + [shift(x, axis, by) for by in STEPS[1:]])


def around_last(x, axis):
    left, right = shift(x, axis, 1), shift(x, axis, -1)
    half = x.shape[0] // 2
    return [x, left, right, shift(left[:half], axis, 1), shift(right[half:], axis, -1)]


def blocks_of(kind, pieces, at_y, at_x):
    if kind == "x, then y":
        return [
            (pieces[0].at[y, j], y, lax.rem(at_x + (8 - STEPS[j]), 4))
            for y in range(NY)
            for j in range(NX)
        ]
    found = []
    for r in range(4):
        for j in range(4):
            if r == 3 and len(pieces) == 3:
                continue
            src = pieces[r].at[j] if r < 3 else pieces[3 + j // 2].at[j % 2]
            y = j if kind == "ordered y, then x" else lax.rem(at_y + (8 - STEPS[j]), 4)
            found.append((src, y, lax.rem(at_x + (8 - STEPS[r]), 4)))
    return found


def turn(sums, cos_ref, sin_ref, out_ref):
    half = HEAD // 2
    for h in range(sums.shape[1] // HEAD):
        vecs = sums[:, h * HEAD : (h + 1) * HEAD]
        turned = jnp.concatenate([vecs[:, half:], vecs[:, :half]], axis=1)
        out_ref[:, h * HEAD : (h + 1) * HEAD] = (
            vecs * cos_ref[...] + turned * sin_ref[...]
        ).astype(jnp.bfloat16)


def pick(rows, x, pairs, out_ref):
    lane = lax.broadcasted_iota(jnp.int32, (512, 128), 1)
    source = (lane >> 5) * 128 + x * 32 + (lane & 31)
    one = (lax.broadcasted_iota(jnp.int32, (512, 128), 0) == source).astype(jnp.float32)
    one = one.astype(jnp.bfloat16)
    for y in range(NY):
        for pair in pairs:
            slabs = [rows[:, pl.ds((z * NY + y) * 256, 256)] for z in (2 * pair, 2 * pair + 1)]
            picked = jnp.dot(
                jnp.concatenate(slabs, axis=1), one, preferred_element_type=jnp.float32
            )
            column = (y * NZ // 2 + pair) * 128
            out_ref[:, column : column + 128] = picked.astype(jnp.bfloat16)


def project_kernel(kinds, counts, partial, place_ref, cos_ref, sin_ref, own_hbm, other_hbm, *refs):
    jobs = len(kinds)
    pieces = [refs[sum(counts[:job]) : sum(counts[: job + 1])] for job in range(jobs)]
    outs = 2 if partial else 1
    out_refs = refs[sum(counts) : sum(counts) + outs]
    rows, accum, rows_sem, sems, weights = refs[sum(counts) + outs :]
    wides = [piece[0].shape[-1] for piece in pieces]
    mine, at_x, at_y = place_ref[0], place_ref[1], place_ref[2]
    tok = own_hbm.shape[0]
    thick = NZ // CHUNKS
    wide_depth = 256 * NY * thick

    def fetch(chunk):
        planes = pl.ds(chunk * thick, thick)
        deep = pl.ds(chunk * wide_depth, wide_depth)
        copies = []
        for job, kind in enumerate(kinds):
            for n, (src, y, x) in enumerate(blocks_of(kind, pieces[job], at_y, at_x)):
                columns = pl.ds(sum(wides[:job]), wides[job])
                dst = weights.at[planes, y, :, x, :, columns]
                copies.append(pltpu.make_async_copy(src.at[planes], dst, sems.at[chunk, job, n]))
        for k, (src, core) in enumerate(((own_hbm, mine), (other_hbm, 1 - mine))):
            dst = rows.at[pl.ds(pl.multiple_of(core * tok, tok), tok), deep]
            copies.append(pltpu.make_async_copy(src.at[:, deep], dst, rows_sem.at[chunk, k]))
        return copies

    far = lax.rem(at_x + (8 - STEPS[3]), 4)
    if partial:
        empty = jnp.zeros((NZ, NY, 2, 1, 32, wides[0]), jnp.bfloat16)
        weights[:, :, :, pl.ds(far, 1), :, : wides[0]] = empty
    chunks = [fetch(chunk) for chunk in range(CHUNKS)]
    for copies in chunks:
        for copy in copies:
            copy.start()
    accum[...] = jnp.zeros(accum.shape, jnp.float32)
    depth = 256 * NY
    for chunk, copies in enumerate(chunks):
        for copy in copies:
            copy.wait()

        @pl.loop(chunk * thick, (chunk + 1) * thick)
        def _(z):
            left = rows[:, pl.ds(pl.multiple_of(z * depth, depth), depth)]
            right = weights[z].reshape(depth, sum(wides))
            accum[...] += jnp.dot(left, right, preferred_element_type=jnp.float32)

        if partial:
            pick(rows, far, range(chunk * thick // 2, (chunk + 1) * thick // 2), out_refs[1])

    if partial:
        out_refs[0][...] = accum[...]
    else:
        turn(accum[...], cos_ref, sin_ref, out_refs[0])


def project(place, tables, own, other, jobs, name, partial=False):
    tok, depth = own.shape
    wides = [pieces[0].shape[-1] for _, pieces in jobs]
    flat = [piece for _, pieces in jobs for piece in pieces]
    vmem = pl.BlockSpec(memory_space=pltpu.VMEM)
    anywhere = pl.BlockSpec(memory_space=pltpu.HBM)
    outs = jax.ShapeDtypeStruct((2 * tok, sum(wides)), jnp.bfloat16)
    if partial:
        outs = (
            jax.ShapeDtypeStruct((2 * tok, sum(wides)), jnp.float32),
            jax.ShapeDtypeStruct((2 * tok, depth // 4), jnp.bfloat16),
        )
    return pl.pallas_call(
        functools.partial(
            project_kernel, [kind for kind, _ in jobs], [len(pieces) for _, pieces in jobs], partial
        ),
        out_shape=outs,
        in_specs=[pl.BlockSpec(memory_space=pltpu.SMEM), vmem, vmem]
        + [anywhere] * (2 + len(flat)),
        out_specs=jax.tree.map(lambda _: vmem, outs),
        scratch_shapes=[
            pltpu.VMEM((2 * tok, depth), jnp.bfloat16),
            pltpu.VMEM((2 * tok, sum(wides)), jnp.float32),
            pltpu.SemaphoreType.DMA((CHUNKS, 2)),
            pltpu.SemaphoreType.DMA((CHUNKS, len(jobs), 16)),
            pltpu.VMEM((NZ, NY, 2, NX, 32, sum(wides)), jnp.bfloat16),
        ],
        compiler_params=pltpu.CompilerParams(vmem_limit_bytes=48 * 2**20),
        cost_estimate=pl.CostEstimate(
            flops=4 * tok * depth * sum(wides),
            bytes_accessed=2 * depth * (2 * tok + sum(wides)),
            transcendentals=0,
        ),
        name=name,
    )(place, *tables, own, other, *flat)


def finish_kernel(cos_ref, sin_ref, sums_ref, rows_ref, first_ref, second_ref, out_ref):
    deep, wide = first_ref.shape
    more = jnp.dot(rows_ref[:, :deep], first_ref[...], preferred_element_type=jnp.float32)
    more += jnp.dot(rows_ref[:, deep:], second_ref[...], preferred_element_type=jnp.float32)
    sums = jnp.concatenate([sums_ref[:, :wide] + more, sums_ref[:, wide:]], axis=1)
    turn(sums, cos_ref, sin_ref, out_ref)


def finish(tables, sums, rows, pieces):
    vmem = pl.BlockSpec(memory_space=pltpu.VMEM)
    return pl.pallas_call(
        finish_kernel,
        out_shape=jax.ShapeDtypeStruct(sums.shape, jnp.bfloat16),
        in_specs=[vmem] * 6,
        out_specs=vmem,
        compiler_params=pltpu.CompilerParams(vmem_limit_bytes=32 * 2**20),
        name="finish_queries",
    )(*tables, sums, rows, *[piece.reshape(-1, piece.shape[-1]) for piece in pieces])


def attend_kernel(heads, span_ref, begin_ref, q_ref, *refs):
    groups = refs[:4]
    out_ref, kv, top, total, accum, sem = refs[4:]
    start, base, low, high, full_low, full_high, mine = [span_ref[i] for i in range(7)]
    tok = q_ref.shape[0]
    factor = np.float32(HEAD**-0.5 * LOG2E)
    copies = []
    for k, src in enumerate(groups):
        which = mine if k < 2 else 1 - mine
        first = 0 if k % 2 == 0 else PLANES - src.shape[1]
        for r in range(4):
            dst = kv.at[which, pl.ds(first, src.shape[1]), r]
            copies.append(pltpu.make_async_copy(src.at[r], dst, sem.at[k, r]))
    for copy in copies[4:8] + copies[12:] + copies[:4] + copies[8:12]:
        copy.start()

    top[...] = jnp.full(top.shape, -1e30, jnp.float32)
    total[...] = jnp.zeros(total.shape, jnp.float32)
    accum[...] = jnp.zeros(accum.shape, jnp.float32)
    for copy in copies[4:8] + copies[12:]:
        copy.wait()
    parts = KB // tok
    rows = NY // parts
    early = rows * groups[0].shape[1]
    ones = jnp.ones((KB, HEAD), jnp.bfloat16)

    def block(i, masked):
        here = pl.ds(lax.rem(i, rows) * parts, parts)
        keys = kv[0, i // rows, here].reshape(KB, HEAD)
        values = jnp.concatenate([kv[1, i // rows, here].reshape(KB, HEAD), ones], axis=1)
        if masked:
            ktok = lax.broadcasted_iota(jnp.int32, (tok, KB), 1) + (base + i * KB)
            qtok = lax.broadcasted_iota(jnp.int32, (tok, KB), 0) + start
            visible = (ktok >= begin_ref[:, 0:1]) & (ktok <= qtok)

        def score(h):
            return lax.dot_general(
                q_ref[:, h * HEAD : (h + 1) * HEAD],
                keys,
                (((1,), (1,)), ((), ())),
                preferred_element_type=jnp.float32,
            )

        following = score(0)
        for h in range(heads):
            scores = following
            if h + 1 < heads:
                following = score(h + 1)
            if masked:
                scores = jnp.where(visible, scores, -1e30)
            old = top[h]
            new = jnp.maximum(old, jnp.max(scores, axis=1, keepdims=True))
            shrink = jnp.exp2((old - new) * factor)
            weights = jnp.exp2((scores - jnp.tile(new, (1, KB // HEAD))) * factor)
            top[h] = new
            sums = jnp.dot(weights.astype(jnp.bfloat16), values, preferred_element_type=jnp.float32)
            total[h] = total[h] * shrink + sums[:, HEAD:]
            accum[h] = accum[h] * shrink + sums[:, :HEAD]

    def wait_early():
        for copy in copies[:4] + copies[8:12]:
            copy.wait()

    @pl.loop(0, high - low)
    def _(n):
        i = high - 1 - n
        full = (i >= full_low) & (i < full_high)

        @pl.when(i == early - 1)
        def _():
            wait_early()

        @pl.when(full)
        def _():
            block(i, False)

        @pl.when(jnp.logical_not(full))
        def _():
            block(i, True)

    @pl.when(low >= early)
    def _():
        wait_early()

    for h in range(heads):
        out_ref[:, h * HEAD : (h + 1) * HEAD] = (accum[h] / total[h]).astype(jnp.bfloat16)


def attend(queries, groups, begins, start, base, mine):
    tok = queries.shape[0]
    heads = queries.shape[1] // HEAD
    spans = jnp.stack(
        [
            start,
            base,
            lax.div(begins[0] - base, KB),
            lax.div(start - base + (tok + KB - 1), KB),
            lax.div(begins[-1] - base + (KB - 1), KB),
            lax.div(start - base + 1, KB),
            mine,
        ]
    ).astype(jnp.int32)
    vmem = pl.BlockSpec(memory_space=pltpu.VMEM)
    state = pltpu.VMEM((heads, tok, HEAD), jnp.float32)
    return pl.pallas_call(
        functools.partial(attend_kernel, heads),
        out_shape=jax.ShapeDtypeStruct((tok, heads * HEAD), jnp.bfloat16),
        in_specs=[pl.BlockSpec(memory_space=pltpu.SMEM), vmem, vmem]
        + [pl.BlockSpec(memory_space=pltpu.HBM)] * 4,
        out_specs=vmem,
        scratch_shapes=[
            pltpu.VMEM((2, PLANES, NY, tok, HEAD), jnp.bfloat16),
            state,
            state,
            state,
            pltpu.SemaphoreType.DMA((4, 4)),
        ],
        compiler_params=pltpu.CompilerParams(vmem_limit_bytes=48 * 2**20),
        name="attend",
    )(spans, jnp.broadcast_to(begins[:, None], (tok, HEAD)), queries, *groups)


def per_device(tokens, projection, doc_lengths):
    half = tokens.shape[1]
    tok = 2 * half
    lengths = doc_lengths[0]
    span = HEADS // 2 * HEAD
    mine, plane = lax.axis_index("core"), lax.axis_index("z")
    at_x, at_y = lax.axis_index("x"), lax.axis_index("y")
    own = tokens[0]
    other = swap(own)

    start = ((plane * NY + at_y) * tok).astype(jnp.int32)
    qtok = start + jnp.arange(tok, dtype=jnp.int32)
    begins = doc_begins(lengths, qtok)
    cosine, sine = turn_tables((qtok - begins).astype(jnp.float32))
    place = jnp.stack([mine, at_x, at_y]).astype(jnp.int32)

    small = jnp.stack([projection[:, 2 * span :][:, :HEAD], projection[:, 2 * span + HEAD :]])
    big = jnp.stack([projection[:, :span], projection[:, span : 2 * span]])
    small = along_chips(small)
    small = around(small, "y")
    big = along_chips(big)
    small, big = lax.optimization_barrier((small, big))
    wide = span * 3 // 4
    most, rest = spread(big[..., :wide], "y"), around(big[..., wide:], "x")
    left, right = shift(small, "x", 1), shift(small, "x", -1)
    left, right, cosine, sine, other = lax.optimization_barrier((left, right, cosine, sine, other))
    halves = [shift(left[:2], "x", 1), shift(right[2:], "x", -1)]
    most, rest, halves = lax.optimization_barrier((most, rest, halves))
    small = [small, left, right] + halves
    most = [most, shift(most, "x", 1), shift(most, "x", -1)]
    distant = [shift(most[1][:2], "x", 1), shift(most[2][2:], "x", -1)]
    rest = [spread(rest, "y")]

    keyed = mine == 0
    tables = jnp.where(keyed, cosine, 1.0), jnp.where(keyed, sine, 0.0)
    keyval = project(place, tables, own, other, [("y, then x", small)], "project_keyval")
    near = [shift(keyval, "z", 2), shift(keyval, "z", 1)]
    far = shift(jnp.stack(near), "z", 2)
    near, rest = lax.optimization_barrier((near + [keyval], rest))
    late = spread(jnp.stack(near), "y")
    far, most[1], most[2] = lax.optimization_barrier((far, most[1], most[2]))
    early = spread(far, "y")
    jobs = [("ordered y, then x", most), ("x, then y", rest)]
    sums, picked = project(place, (cosine, sine), own, other, jobs, "project_queries", True)
    early, late, distant, sums = lax.optimization_barrier((early, late, distant, sums))
    groups = [early, late, swap(early), swap(late)]
    queries = finish((cosine, sine), sums, picked, distant)
    base = ((plane - (PLANES - 1)) * (NY * tok)).astype(jnp.int32)
    mixed = attend(queries, groups, begins, start, base, mine).reshape(2, half, span)
    kept = lax.dynamic_index_in_dim(mixed, mine, 0, keepdims=False)
    given = swap(lax.dynamic_index_in_dim(mixed, 1 - mine, 0, keepdims=False))
    return jnp.where(
        keyed, jnp.concatenate([kept, given], axis=1), jnp.concatenate([given, kept], axis=1)
    )[None]


def solution(mesh):
    mesh = Mesh(mesh.devices.reshape(NZ, NY, 2, NX), ("z", "y", "core", "x"))
    everyone = ("z", "y", "core")
    in_specs = (P("x", everyone, None), P(everyone + ("x",), None), P("x", None))
    out_specs = P("x", everyone, None)
    return jax.shard_map(
        per_device, mesh=mesh, in_specs=in_specs, out_specs=out_specs, check_vma=False
    )
```
